768 devices in a mesh: ctx: 48 (over y_lo, z), head: 16 (over y_hi, x, core).
Axes of the slice: x: 4, y: 8 (y_hi: 2, y_lo: 4; y = y_hi * 4 + y_lo), z: 12, core: 2. Of those that a mesh axis runs over, the one named last changes fastest.
Arguments:
- enc_states: bfloat16 [49152, 1024], P('ctx'), may hold values from -6 to 6
- local_gain: float32 [1024], replicated, may hold values from 0.1 to 1.9
- w_local: bfloat16 [1024, 16, 192], P(None, 'head'), may hold values from -10 to 10
- w_cross: bfloat16 [16, 64, 320], P('head'), may hold values from -50 to 50
- w_patch: bfloat16 [16, 64, 256], P('head'), may hold values from -0.75 to 0.75
- byte_patch: int32 [49152], P('ctx'), may hold values from 0 to 6143, as said below
- global_gain: float32 [4096], replicated, may hold values from 0.1 to 1.9
- w_global: bfloat16 [4096, 32, 384], P(None, 'head'), may hold values from -6 to 6
Outputs:
- context: bfloat16 [6144, 4096], P('ctx', 'head')
The draws below stay inside these ranges and needn't reach their ends.
Inputs may be any that keep to these rules, and one draw needn't show every extreme that they name: byte_patch never falls and rises by at most one from byte to byte; every slab of 1024 bytes starts a new patch; the first patch of slab c has an index in [c * 128, (c + 1) * 128), so a slab holds 1 to 255 patches and both ends are reached; the first byte is in patch 0 and the last in patch 6144 - 1.
All inputs are finite; a program needn't handle non-finite values.
Results may differ from the reference program's by a relative error of at most 0.0095.
The reference program's roundings to bfloat16 on the way (of `normed`, `local_proj`, `local_out`, `cross_proj`, `pooled`, `patch_rows`, `scaled_rows` and `global_proj`) count: a program that leaves them out, or rounds other values in their place, can miss the bound.
Values may be sent and summed in bfloat16 or wider, within the bound.
No kernel may reach another device: no remote copies, remote signals or barrier semaphores. Data moves between devices by JAX's collectives and lax.ppermute only.
A program may use at most 64 MiB of HBM per device.

```python
import math
import jax
import jax.numpy as jnp
from jax import lax

HL = 16
DH_L = 64
HG = 32
DH = 128
W = 512
B_DEV = 1024
DL = 1024
DG = 4096
LIFT = 256
P_DEV = 128
BYTES = 49152
PATCHES = 6144
N_CTX = 48


def drawn_projection(key, fan_in, head_total, head_size):
    first_key = jax.random.fold_in(key, 0)
    limit = math.sqrt(3.0) / math.sqrt(fan_in)
    base = jax.random.uniform(first_key, (fan_in, head_total, 3 * head_size), jnp.float32, -limit, limit)
    queries = base[:, :, :head_size]
    own_keys = base[:, :, head_size:2 * head_size]
    values = base[:, :, 2 * head_size:]
    return jnp.concatenate([queries, own_keys, values], axis=-1)


def draw_w_local(key, part):
    return drawn_projection(jax.random.fold_in(key, 11), DL, HL, DH_L).astype(jnp.bfloat16)


def draw_w_global(key, part):
    return drawn_projection(jax.random.fold_in(key, 13), DG, HG, DH).astype(jnp.bfloat16)


def draw_w_cross(key, part):
    first_key = jax.random.fold_in(jax.random.fold_in(key, 19), 0)
    limit = math.sqrt(3.0) / math.sqrt(DH_L)
    base = jax.random.uniform(first_key, (HL, DH_L, DH_L + LIFT), jnp.float32, -limit, limit)
    key_part = base[:, :, :DH_L]
    value_part = base[:, :, DH_L:]
    return jnp.concatenate([key_part, value_part], axis=-1).astype(jnp.bfloat16)


def draw_byte_patch(key, part):
    excess_key, cut_key = jax.random.split(jax.random.fold_in(key, 17))
    excess = jax.random.randint(excess_key, (N_CTX + 1,), 0, P_DEV)
    places = jnp.arange(N_CTX + 1, dtype=jnp.int32)
    excess = jnp.where((places == 0) | (places == N_CTX) | (places == 2), 0, excess)
    excess = jnp.where(places == 1, P_DEV - 1, excess).astype(jnp.int32)
    firsts = jnp.arange(N_CTX, dtype=jnp.int32) * P_DEV + excess[:N_CTX]
    patch_counts = P_DEV + excess[1:] - excess[:N_CTX]
    slab_keys = jax.random.split(cut_key, N_CTX)
    orders = jax.vmap(lambda one_key: jax.random.permutation(one_key, B_DEV - 1))(slab_keys)
    ranks = jnp.argsort(orders, axis=1).astype(jnp.int32)
    cuts = (ranks < (patch_counts - 1)[:, None]).astype(jnp.int32)
    cuts = jnp.concatenate([jnp.zeros((N_CTX, 1), jnp.int32), cuts], axis=1)
    return (firsts[:, None] + jnp.cumsum(cuts, axis=1)).astype(jnp.int32).reshape(-1)


def level_of(own_key, extent, cuts, smallest, top_value):
    factor_of, own = 1.0, jax.random.fold_in(own_key, 6)
    for axis_at, blocks in cuts:
        steps = jnp.exp(jax.random.uniform(jax.random.fold_in(own, axis_at), (blocks,), jnp.float32, smallest / len(cuts), top_value / len(cuts)))
        factor_of = factor_of * jnp.repeat(steps, extent[axis_at] // blocks).reshape([-1 if axis == axis_at else 1 for axis in range(len(extent))])
    return factor_of


def bell_draw(rng, shape, deviation, most, cuts=(), kind=jnp.bfloat16):
    drawn = deviation * jax.random.normal(rng, shape, jnp.float32)
    if cuts:
        drawn = drawn * level_of(rng, shape, cuts, -0.22, 0.18)
    return jnp.clip(drawn, -most, most).astype(kind)


def setup_inputs(seed: int = 0) -> dict:
    key_of = jax.random.split(jax.random.key(seed), 9)
    return {
        "enc_states": bell_draw(key_of[0], (BYTES, DL), 1.0, 6.0, ((0, 48),)),
        "local_gain": jnp.clip(1.0 + 0.18 * jax.random.normal(key_of[1], (DL,), jnp.float32), 0.1, 1.9),
        "w_local": draw_w_local(jax.random.fold_in(key_of[8], 71), 0),
        "w_cross": draw_w_cross(jax.random.fold_in(key_of[8], 71), 0),
        "w_patch": bell_draw(key_of[4], (HL, DH_L, LIFT), DH_L ** -0.5, 0.75, ((0, 16),)),
        "byte_patch": draw_byte_patch(jax.random.fold_in(key_of[8], 71), 0),
        "global_gain": jnp.clip(1.0 + 0.18 * jax.random.normal(key_of[6], (DG,), jnp.float32), 0.1, 1.9),
        "w_global": draw_w_global(jax.random.fold_in(key_of[8], 71), 0),
    }


neg_large = -1e+30

def masked_softmax_apply(scores, allowed, values):
    row_peak = lax.optimization_barrier(jnp.max(jnp.where(allowed, scores, neg_large), axis=-1, keepdims=True))
    weights = jnp.where(allowed, jnp.exp(scores - row_peak), 0.0)
    normalizer = lax.optimization_barrier(jnp.sum(weights, axis=-1))
    normalizer = jnp.where(normalizer > 0, normalizer, 1.0)
    rounded = lax.optimization_barrier(weights.astype(jnp.bfloat16)).astype(jnp.float32)
    summed = jnp.einsum('hqk,khd->qhd', rounded, values.astype(jnp.float32))
    return summed / jnp.transpose(normalizer)[:, :, None]

def window_attend(queries, keys_vals, anchor):
    head_size = queries.shape[-1]
    scores = jnp.einsum('qhd,khd->hqk', queries.astype(jnp.float32), keys_vals[:, :, :head_size].astype(jnp.float32)) / math.sqrt(head_size)
    rows_at = lax.broadcasted_iota(jnp.int32, scores.shape, 1)
    cols_at = lax.broadcasted_iota(jnp.int32, scores.shape, 2)
    window = keys_vals.shape[0] - queries.shape[0]
    allowed = (cols_at > rows_at) & (cols_at <= rows_at + window) & (anchor + cols_at - window >= 0)
    return masked_softmax_apply(scores, allowed, keys_vals[:, :, head_size:])

def cross_attend(outputs, patch_ids, cross_weight, patch_weight, slot_count):
    head_size = outputs.shape[-1]
    first_id = patch_ids[0]
    local_ids = patch_ids - first_id
    member = local_ids[None, :] == jnp.arange(slot_count, dtype=jnp.int32)[:, None]
    member_f = member.astype(jnp.float32)
    counts = lax.optimization_barrier(jnp.sum(member_f, axis=1))
    pooled = (jnp.einsum('pb,bhd->phd', member_f, outputs.astype(jnp.float32)) / jnp.maximum(counts, 1.0)[:, None, None]).astype(jnp.bfloat16)
    cross_proj = jnp.einsum('bhd,hde->bhe', outputs.astype(jnp.float32), cross_weight.astype(jnp.float32)).astype(jnp.bfloat16)
    scores = jnp.einsum('phd,bhd->hpb', pooled.astype(jnp.float32), cross_proj[:, :, :head_size].astype(jnp.float32)) / math.sqrt(head_size)
    allowed = jnp.broadcast_to(member[None], scores.shape)
    attended = masked_softmax_apply(scores, allowed, cross_proj[:, :, head_size:])
    lifted = jnp.einsum('phd,hde->phe', pooled.astype(jnp.float32), patch_weight.astype(jnp.float32))
    patch_rows = (lifted + attended).astype(jnp.bfloat16)
    return (patch_rows.reshape(slot_count, -1), first_id, patch_ids[-1] - first_id + 1)

def reference(enc_states, local_gain, w_local, w_cross, w_patch, byte_patch, global_gain, w_global):
    states = enc_states.astype(jnp.float32)
    normed = (states * lax.rsqrt(lax.optimization_barrier(jnp.mean(states * states, axis=-1, keepdims=True)) + 1e-05) * local_gain).astype(jnp.bfloat16)
    local_proj = jnp.einsum('bd,dhe->bhe', normed.astype(jnp.float32), w_local.astype(jnp.float32)).astype(jnp.bfloat16)
    block_rows = min(512, B_DEV)
    padded = jnp.concatenate([jnp.zeros((W, HL, 2 * DH_L), jnp.bfloat16), local_proj[:, :, DH_L:]], axis=0)

    def one_block(block_index):
        first_row = (block_index * block_rows).astype(jnp.int32)
        queries = lax.dynamic_slice_in_dim(local_proj[:, :, :DH_L], first_row, block_rows, 0)
        keys_vals = lax.dynamic_slice_in_dim(padded, first_row, block_rows + W, 0)
        return window_attend(queries, keys_vals, first_row).astype(jnp.bfloat16)
    local_out = lax.map(one_block, jnp.arange(BYTES // block_rows, dtype=jnp.int32)).reshape(BYTES, HL, DH_L)
    slot_count = 2 * P_DEV

    def one_slab(pieces):
        return cross_attend(pieces[0], pieces[1], w_cross, w_patch, slot_count)
    slab_rows, firsts, patch_counts = lax.map(one_slab, (local_out.reshape(N_CTX, B_DEV, HL, DH_L), byte_patch.reshape(N_CTX, B_DEV)))
    offsets = jnp.arange(slot_count, dtype=jnp.int32)[None, :]
    targets = jnp.where(offsets < patch_counts[:, None], firsts[:, None] + offsets, PATCHES).astype(jnp.int32).reshape(-1)
    patch_rows = jnp.zeros((PATCHES + 1, DG), jnp.bfloat16).at[targets].set(slab_rows.reshape(-1, DG))[:PATCHES]
    rows_f = patch_rows.astype(jnp.float32)
    row_scale = lax.rsqrt(lax.optimization_barrier(jnp.mean(rows_f * rows_f, axis=-1)) + 1e-05)
    scaled_rows = (rows_f * global_gain).astype(jnp.bfloat16)
    global_proj = (jnp.dot(scaled_rows, w_global.reshape(DG, HG * 3 * DH), preferred_element_type=jnp.float32) * row_scale[:, None]).astype(jnp.bfloat16).reshape(PATCHES, HG, 3 * DH)

    def one_query_block(block_index):
        first_row = (block_index * P_DEV).astype(jnp.int32)
        queries = lax.dynamic_slice_in_dim(global_proj[:, :, :DH], first_row, P_DEV, 0)
        scores = jnp.einsum('qhd,khd->hqk', queries.astype(jnp.float32), global_proj[:, :, DH:2 * DH].astype(jnp.float32)) / math.sqrt(DH)
        rows_at = first_row + lax.broadcasted_iota(jnp.int32, scores.shape, 1)
        cols_at = lax.broadcasted_iota(jnp.int32, scores.shape, 2)
        return masked_softmax_apply(scores, cols_at <= rows_at, global_proj[:, :, 2 * DH:]).astype(jnp.bfloat16)
    context = lax.map(one_query_block, jnp.arange(N_CTX, dtype=jnp.int32)).reshape(PATCHES, HG * DH)
    return context
```

```python
import functools
import math

import jax
import jax.numpy as jnp
from jax import lax
from jax.experimental import pallas as pl
from jax.experimental.pallas import tpu as pltpu
from jax.sharding import Mesh, PartitionSpec as P

CTX = ("yl", "zh", "zl")
HEAD = ("yh", "x", "core")
Y_LO, Z_HALF, Z_PAIR, Y_HI, X, CORE = 4, 6, 2, 2, 4, 2
N_CTX = Y_LO * Z_HALF * Z_PAIR

DH_L = 64
DH = 128
W = 512
PATCH_LEN = 8
DG = 4096


neg_large = -1e30


def passed_along(block, axis, distance):
    devices = range(N_CTX)
    route = [(i - distance, i) for i in devices if i - distance in devices]
    return lax.ppermute(block, axis, route)


def masked_softmax_apply(scores, allowed, values):
    row_peak = jnp.max(jnp.where(allowed, scores, neg_large), axis=-1, keepdims=True)
    weights = jnp.where(allowed, jnp.exp(scores - row_peak), 0.0)
    normalizer = jnp.sum(weights, axis=-1)
    normalizer = jnp.where(normalizer > 0, normalizer, 1.0)
    summed = jnp.einsum(
        "hqk,khd->qhd", weights.astype(jnp.bfloat16), values, preferred_element_type=jnp.float32
    )
    return summed / jnp.transpose(normalizer)[:, :, None]


def window_attend(queries, keys_vals, anchor):
    head_size = queries.shape[-1]
    scores = jnp.einsum(
        "qhd,khd->hqk", queries, keys_vals[:, :, :head_size], preferred_element_type=jnp.float32
    ) / math.sqrt(head_size)
    rows_at = lax.broadcasted_iota(jnp.int32, scores.shape, 1)
    cols_at = lax.broadcasted_iota(jnp.int32, scores.shape, 2)
    window = keys_vals.shape[0] - queries.shape[0]
    allowed = (cols_at > rows_at) & (cols_at <= rows_at + window) & (anchor + cols_at - window >= 0)
    return masked_softmax_apply(scores, allowed, keys_vals[:, :, head_size:])


def cross_attend(outputs, patch_ids, cross_weight, patch_weight, slot_count):
    head_size = outputs.shape[-1]
    first_id = patch_ids[0]
    local_ids = patch_ids - first_id
    member = local_ids[None, :] == jnp.arange(slot_count, dtype=jnp.int32)[:, None]
    counts = jnp.sum(member.astype(jnp.float32), axis=1)
    pooled = (
        jnp.einsum(
            "pb,bhd->phd", member.astype(jnp.bfloat16), outputs, preferred_element_type=jnp.float32
        )
        / jnp.maximum(counts, 1.0)[:, None, None]
    ).astype(jnp.bfloat16)
    cross_proj = jnp.einsum(
        "bhd,hde->bhe", outputs, cross_weight, preferred_element_type=jnp.float32
    ).astype(jnp.bfloat16)
    scores = jnp.einsum(
        "phd,bhd->hpb", pooled, cross_proj[:, :, :head_size], preferred_element_type=jnp.float32
    ) / math.sqrt(head_size)
    allowed = member[None]
    attended = masked_softmax_apply(scores, allowed, cross_proj[:, :, head_size:])
    lifted = jnp.einsum("phd,hde->phe", pooled, patch_weight, preferred_element_type=jnp.float32)
    patch_rows = (lifted + attended).astype(jnp.bfloat16)
    return (patch_rows.reshape(slot_count, -1), first_id, patch_ids[-1] - first_id + 1)


def project_kernel(pos_ref, own_ref, other_ref, gain_ref, w_ref, out_ref):
    core = pos_ref[2]
    rows = own_ref.shape[2]
    width = own_ref.shape[3]
    total = jnp.zeros((rows, w_ref.shape[1]), jnp.float32)
    squares = jnp.zeros((rows, 1), jnp.float32)
    for block_ref, block_core in ((own_ref, core), (other_ref, 1 - core)):
        for x in range(X):
            for yh in range(Y_HI):
                block = block_ref[x, yh].astype(jnp.float32)
                first = pl.multiple_of((yh * X * CORE + x * CORE + block_core) * width, width)
                gain = gain_ref[:, pl.ds(first, width)]
                squares = squares + jnp.sum(block * block, axis=1, keepdims=True)
                total = total + jnp.dot(
                    (block * gain).astype(jnp.bfloat16),
                    w_ref[pl.ds(first, width), :],
                    preferred_element_type=jnp.float32,
                )
    out_ref[...] = (total * lax.rsqrt(squares / DG + 1e-05)).astype(jnp.bfloat16)


def attend_kernel(pos_ref, q_ref, kv_ref, out_ref, vt_ref, s_ref):
    y = pos_ref[0]
    zh = pos_ref[1]
    key_count = kv_ref.shape[0]
    rows = 2 * q_ref.shape[1]
    half = q_ref.shape[1]
    scale = math.log2(math.e) / math.sqrt(DH)
    vt_ref[...] = kv_ref[:, DH:].T
    chunk = 512

    def attend(yy, masked):
        queries = q_ref[pl.ds(2 * yy, 2)].reshape(rows, DH)
        peak = jnp.full((1, rows), neg_large, jnp.float32)
        for first in range(0, key_count, chunk):
            scores = lax.dot_general(
                kv_ref[first : first + chunk, :DH],
                queries,
                (((1,), (1,)), ((), ())),
                preferred_element_type=jnp.float32,
            ) * scale
            if masked:
                key_at = first + lax.broadcasted_iota(jnp.int32, scores.shape, 0)
                query_at = zh * rows + lax.broadcasted_iota(jnp.int32, scores.shape, 1)
                scores = jnp.where(key_at <= query_at, scores, neg_large)
            s_ref[first : first + chunk] = scores
            peak = jnp.maximum(peak, jnp.max(scores, axis=0, keepdims=True))
        normalizer = jnp.zeros((1, rows), jnp.float32)
        summed = jnp.zeros((DH, rows), jnp.float32)
        for first in range(0, key_count, chunk):
            weights = jnp.exp2(s_ref[first : first + chunk] - peak)
            normalizer = normalizer + jnp.sum(weights, axis=0, keepdims=True)
            summed = summed + jnp.dot(
                vt_ref[:, first : first + chunk],
                weights.astype(jnp.bfloat16),
                preferred_element_type=jnp.float32,
            )
        summed = (summed / normalizer).astype(jnp.bfloat16)
        level = peak + jnp.log2(normalizer)
        high = level.astype(jnp.bfloat16)
        rest = level - high.astype(jnp.float32)
        mid = rest.astype(jnp.bfloat16)
        low = (rest - mid.astype(jnp.float32)).astype(jnp.bfloat16)
        stats = jnp.concatenate(
            [high, mid, low, jnp.zeros((13, rows), jnp.bfloat16)], axis=0
        )
        for part in range(2):
            lanes = slice(part * half, (part + 1) * half)
            out_ref[2 * yy + part, :DH, :] = summed[:, lanes]
            out_ref[2 * yy + part, DH:, :] = stats[:, lanes]

    for yy in range(Y_LO):

        @pl.when(yy < y)
        def _():
            row_at = lax.broadcasted_iota(jnp.int32, (16, half), 0)
            stats = jnp.where(row_at == 0, neg_large, 0.0).astype(jnp.bfloat16)
            for part in range(2):
                out_ref[2 * yy + part, :DH, :] = jnp.zeros((DH, half), jnp.bfloat16)
                out_ref[2 * yy + part, DH:, :] = stats

        @pl.when(yy == y)
        def _():
            attend(yy, True)

        @pl.when(yy > y)
        def _():
            attend(yy, False)


def merge_kernel(parts_ref, out_ref):
    for head in range(2):
        levels = []
        for yy in range(Y_LO):
            stats = parts_ref[2 * yy + head, DH:, :].astype(jnp.float32)
            levels.append(stats[0:1] + stats[1:2] + stats[2:3])
        peak = functools.reduce(jnp.maximum, levels)
        total = jnp.zeros((DH, out_ref.shape[0]), jnp.float32)
        normalizer = jnp.zeros((1, out_ref.shape[0]), jnp.float32)
        for yy in range(Y_LO):
            share = jnp.exp2(levels[yy] - peak)
            normalizer = normalizer + share
            total = total + share * parts_ref[2 * yy + head, :DH, :].astype(jnp.float32)
        out_ref[:, head * DH : (head + 1) * DH] = (total / normalizer).T.astype(jnp.bfloat16)


VMEM = pl.BlockSpec(memory_space=pltpu.VMEM)
SMEM = pl.BlockSpec(memory_space=pltpu.SMEM)


def all_to_all_of(block, axes):
    return lax.all_to_all(block, axes, 0, 0, tiled=True)


def local(enc_states, local_gain, w_local, w_cross, w_patch, byte_patch, global_gain, w_global):
    byte_count = enc_states.shape[0]
    quota = byte_count // PATCH_LEN
    ctx_pos = lax.axis_index(CTX)
    states = enc_states.astype(jnp.float32)
    normed = (
        states * lax.rsqrt(jnp.mean(states * states, axis=-1, keepdims=True) + 1e-05) * local_gain
    ).astype(jnp.bfloat16)
    local_proj = jnp.einsum(
        "bd,dhe->bhe", normed, w_local, preferred_element_type=jnp.float32
    ).astype(jnp.bfloat16)
    rim_rows = passed_along(local_proj[byte_count - W :, :, DH_L:], CTX, 1)
    keys_all = jnp.concatenate([rim_rows, local_proj[:, :, DH_L:]], axis=0)
    block_rows = min(512, byte_count)
    outputs_list = []
    for first_row in range(0, byte_count, block_rows):
        attended = window_attend(
            local_proj[first_row : first_row + block_rows, :, :DH_L],
            keys_all[first_row : first_row + block_rows + W],
            ctx_pos * byte_count + first_row,
        )
        outputs_list.append(attended.astype(jnp.bfloat16))
    local_out = jnp.concatenate(outputs_list, axis=0)
    slot_count = 2 * quota
    local_rows, first_id, patch_count = cross_attend(
        local_out, byte_patch, w_cross, w_patch, slot_count
    )
    slot_index = jnp.arange(slot_count, dtype=jnp.int32)[:, None]
    local_rows = jnp.where(slot_index < patch_count, local_rows, jnp.zeros_like(local_rows))
    excess = first_id - ctx_pos * quota
    padded = jnp.concatenate(
        [jnp.zeros((quota, local_rows.shape[1]), jnp.bfloat16), local_rows], axis=0
    )
    kept_rows = lax.dynamic_slice_in_dim(padded, quota - excess, quota, 0)
    leaving = lax.dynamic_slice_in_dim(local_rows, quota - excess, quota, 0)
    arriving = passed_along(leaving, CTX, 1)
    slab_rows = kept_rows + arriving
    head_total = w_global.shape[1]
    flat_weight = w_global.reshape(DG, head_total * 3 * DH)
    y = lax.axis_index("yl")
    zh = lax.axis_index("zh")
    zl = lax.axis_index("zl")
    pos = jnp.stack([y, zh, lax.axis_index("core")]).astype(jnp.int32)
    pair_rows = lax.all_gather(slab_rows, "yh", axis=0)
    own_rows = all_to_all_of(jnp.broadcast_to(pair_rows[None], (X,) + pair_rows.shape), "x")
    other_rows = lax.ppermute(own_rows, "core", [(0, 1), (1, 0)])
    global_proj = pl.pallas_call(
        project_kernel,
        out_shape=jax.ShapeDtypeStruct((quota, head_total * 3 * DH), jnp.bfloat16),
        in_specs=[SMEM, VMEM, VMEM, VMEM, VMEM],
        out_specs=VMEM,
        compiler_params=pltpu.CompilerParams(vmem_limit_bytes=32 << 20),
        cost_estimate=pl.CostEstimate(
            flops=2 * quota * DG * head_total * 3 * DH, bytes_accessed=8 << 20, transcendentals=0
        ),
        name="project",
    )(pos, own_rows, other_rows, global_gain.reshape(1, DG), flat_weight)
    first_kv = global_proj[:, DH : 3 * DH]
    second_kv = global_proj[:, 4 * DH : 6 * DH]
    swapped = lax.ppermute(jnp.where(zl == 0, second_kv, first_kv), "zl", [(0, 1), (1, 0)])
    queries = jnp.stack([global_proj[:, :DH], global_proj[:, 3 * DH : 4 * DH]])
    queries = jnp.broadcast_to(queries[None], (Y_LO,) + queries.shape)
    queries = queries.reshape(Y_LO * Z_PAIR, quota, DH)
    queries = all_to_all_of(queries, ("yl", "zl"))
    pair_kv = jnp.concatenate(
        [jnp.where(zl == 0, first_kv, swapped), jnp.where(zl == 0, swapped, second_kv)], axis=0
    )
    keys_vals = lax.all_gather(pair_kv, "zh", axis=0, tiled=True)
    key_count = keys_vals.shape[0]
    partial_out = pl.pallas_call(
        attend_kernel,
        out_shape=jax.ShapeDtypeStruct((Y_LO * Z_PAIR, DH + 16, quota), jnp.bfloat16),
        in_specs=[SMEM, VMEM, VMEM],
        out_specs=VMEM,
        scratch_shapes=[
            pltpu.VMEM((DH, key_count), jnp.bfloat16),
            pltpu.VMEM((key_count, 2 * quota), jnp.float32),
        ],
        compiler_params=pltpu.CompilerParams(vmem_limit_bytes=32 << 20),
        name="attend",
    )(pos, queries, keys_vals)
    parts = all_to_all_of(partial_out, ("yl", "zl"))
    return pl.pallas_call(
        merge_kernel,
        out_shape=jax.ShapeDtypeStruct((quota, head_total * DH), jnp.bfloat16),
        in_specs=[VMEM],
        out_specs=VMEM,
        name="merge",
    )(parts)


def solution(mesh):
    split = Mesh(
        mesh.devices.reshape(Y_LO, Z_HALF, Z_PAIR, Y_HI, X, CORE), CTX + HEAD
    )
    in_specs = (
        P(CTX, None),
        P(),
        P(None, HEAD, None),
        P(HEAD, None, None),
        P(HEAD, None, None),
        P(CTX),
        P(),
        P(None, HEAD, None),
    )
    out_specs = P(CTX, HEAD)
    return jax.shard_map(local, mesh=split, in_specs=in_specs, out_specs=out_specs, check_vma=False)
```

```python
import functools
import math

import jax
import jax.numpy as jnp
from jax import lax
from jax.experimental import pallas as pl
from jax.experimental.pallas import tpu as pltpu
from jax.sharding import Mesh, PartitionSpec as P

CTX = ("yl", "zh", "zl")
HEAD = ("yh", "x", "core")
Y_LO, Z_HALF, Z_PAIR, Y_HI, X, CORE = 4, 6, 2, 2, 4, 2
N_CTX = Y_LO * Z_HALF * Z_PAIR

DH_L = 64
DH = 128
PATCH_LEN = 8
DG = 4096


neg_large = -1e30


def passed_along(block, axis, distance):
    devices = range(N_CTX)
    route = [(i - distance, i) for i in devices if i - distance in devices]
    return lax.ppermute(block, axis, route)


def rows_arriving(states_ref, held_ref, sems, first_row):
    step = held_ref.shape[1]
    copies = []
    for part in range(held_ref.shape[0]):
        rows = pl.ds(first_row + part * step, step)
        copy = pltpu.make_async_copy(states_ref.at[rows], held_ref.at[part], sems.at[part])
        copy.start()
        copies.append(copy)
    return copies


def norm_rows(states_ref, gain_ref, normed_ref):
    step = 32
    gain = gain_ref[...]
    for first in range(0, states_ref.shape[0], step):
        states = states_ref[first : first + step].astype(jnp.float32)
        scale = lax.rsqrt(jnp.mean(states * states, axis=1, keepdims=True) + 1e-05)
        normed_ref[first : first + step] = (states * scale * gain).astype(jnp.bfloat16)


def project_rows(weight_ref, normed_ref):
    return lax.dot_general(
        weight_ref[...], normed_ref[...], (((1,), (1,)), ((), ())), preferred_element_type=jnp.float32
    ).astype(jnp.bfloat16)


def second_half_kernel(
    states_ref, gain_hbm, w_hbm, query_ref, rim_ref, held_ref, normed_ref, gain_ref, w_ref, sems
):
    half = query_ref.shape[1]
    parts = held_ref.shape[0]
    gain_copy = pltpu.make_async_copy(gain_hbm, gain_ref, sems.at[parts])
    gain_copy.start()
    copies = rows_arriving(states_ref, held_ref, sems, half)
    w_copy = pltpu.make_async_copy(w_hbm, w_ref, sems.at[parts + 1])
    w_copy.start()
    gain_copy.wait()
    step = held_ref.shape[1]
    for part, copy in enumerate(copies):
        copy.wait()
        norm_rows(held_ref.at[part], gain_ref, normed_ref.at[pl.ds(part * step, step)])
    w_copy.wait()
    proj = project_rows(w_ref, normed_ref)
    query_ref[...] = proj[:DH_L]
    rim_ref[...] = proj[DH_L:]


def window_attend(queries_t, keys_ref, values_ref, early_bias, out_ref):
    scale = 1.0 / math.sqrt(DH_L)
    width = 128
    blocks = range(queries_t.shape[1] // width)
    row_at = lax.broadcasted_iota(jnp.int32, (width, width), 0)
    col_at = lax.broadcasted_iota(jnp.int32, (width, width), 1)
    scores = []
    for block in blocks:
        block_scores = []
        queries = queries_t[:, block * width : (block + 1) * width]
        for part in range(5):
            at = (block + part) * width
            part_scores = jnp.dot(
                keys_ref[at : at + width], queries, preferred_element_type=jnp.float32
            )
            if part == 0:
                part_scores = jnp.where(row_at > col_at, part_scores, neg_large)
            if part == 4:
                part_scores = jnp.where(row_at <= col_at, part_scores, neg_large)
            if early_bias is not None and at < keys_ref.shape[0] // 2:
                part_scores = part_scores + early_bias
            block_scores.append(part_scores)
        scores.append(block_scores)
    weights = []
    normalizers = []
    for block in blocks:
        peak = jnp.max(functools.reduce(jnp.maximum, scores[block]), axis=0, keepdims=True)
        block_weights = [jnp.exp((part_scores - peak) * scale) for part_scores in scores[block]]
        normalizers.append(
            jnp.sum(functools.reduce(jnp.add, block_weights), axis=0, keepdims=True)
        )
        weights.append(
            jnp.concatenate([part.astype(jnp.bfloat16) for part in block_weights], axis=0)
        )
    summed = [
        jnp.dot(
            values_ref[:, block * width : (block + 5) * width],
            weights[block],
            preferred_element_type=jnp.float32,
        )
        for block in blocks
    ]
    for block in blocks:
        out_ref[block * width : (block + 1) * width] = (
            summed[block] / normalizers[block]
        ).T.astype(jnp.bfloat16)


def started(pairs, sems, first):
    copies = [
        pltpu.make_async_copy(source, target, sems.at[first + at])
        for at, (source, target) in enumerate(pairs)
    ]
    for copy in copies:
        copy.start()
    return copies


def first_half_kernel(
    states_ref, gain_hbm, w_hbm, query_hbm, second_hbm, first_ref, out_ref,
    held_ref, normed_ref, gain_ref, w_ref, query_ref, second_ref, keys_ref, values_ref, sems,
):
    half = first_ref.shape[1]
    parts = held_ref.shape[0]
    step = held_ref.shape[1]
    (gain_copy,) = started(((gain_hbm, gain_ref),), sems, parts)
    copies = rows_arriving(states_ref, held_ref, sems, 0)
    others = started(
        ((second_hbm, second_ref), (w_hbm, w_ref), (query_hbm, query_ref)), sems, parts + 1
    )
    gain_copy.wait()
    for part, copy in enumerate(copies):
        copy.wait()
        norm_rows(held_ref.at[part], gain_ref, normed_ref.at[pl.ds(part * step, step)])
    for copy in others:
        copy.wait()
    keys_ref[half:] = second_ref[:DH_L].T
    values_ref[:, half:] = second_ref[DH_L:]
    proj = project_rows(w_ref, normed_ref)
    first_ref[...] = proj
    keys_ref[:half] = proj[DH_L : 2 * DH_L].T
    values_ref[:, :half] = proj[2 * DH_L :]
    window_attend(query_ref[...], keys_ref, values_ref, None, out_ref)


def patch_kernel(
    rim_hbm, first_hbm, late_hbm, patch_hbm, cross_hbm, lift_hbm, kept_ref, leaving_ref,
    rim_ref, first_ref, patch_ref, cross_ref, lift_ref, keys_ref, values_ref, local_ref, sems,
):
    ctx = lax.axis_index(CTX)
    half = first_ref.shape[1]
    copies = started(
        (
            (rim_hbm, rim_ref),
            (first_hbm, first_ref),
            (late_hbm, local_ref.at[pl.ds(half, half)]),
            (patch_hbm, patch_ref),
            (cross_hbm, cross_ref),
            (lift_hbm, lift_ref),
        ),
        sems,
        0,
    )
    for copy in copies:
        copy.wait()
    rim_bias = jnp.where(ctx > 0, 0.0, neg_large).astype(jnp.float32)
    keys_ref[:half] = rim_ref[:DH_L].T
    keys_ref[half:] = first_ref[DH_L : 2 * DH_L].T
    values_ref[:, :half] = rim_ref[DH_L:]
    values_ref[:, half:] = first_ref[2 * DH_L :]
    window_attend(first_ref[:DH_L], keys_ref, values_ref, rim_bias, local_ref)
    local_out = local_ref[...]
    quota = kept_ref.shape[0]
    slots = 2 * quota
    slot_of = patch_ref[...] - ctx * quota
    member = slot_of == lax.broadcasted_iota(jnp.int32, (slots, 2 * half), 0)
    member_f = jnp.where(member, 1.0, 0.0)
    counts = jnp.sum(member_f, axis=1, keepdims=True)
    pooled = (
        jnp.dot(member_f.astype(jnp.bfloat16), local_out, preferred_element_type=jnp.float32)
        / jnp.maximum(counts, 1.0)
    ).astype(jnp.bfloat16)
    keys = jnp.dot(
        local_out, cross_ref[:, :DH_L], preferred_element_type=jnp.float32
    ).astype(jnp.bfloat16)
    values = jnp.dot(
        local_out, cross_ref[:, DH_L:], preferred_element_type=jnp.float32
    ).astype(jnp.bfloat16)
    scores = lax.dot_general(
        pooled, keys, (((1,), (1,)), ((), ())), preferred_element_type=jnp.float32
    )
    scores = jnp.where(member, scores, neg_large)
    peak = jnp.max(scores, axis=1, keepdims=True)
    weights = jnp.where(member, jnp.exp((scores - peak) * (1.0 / math.sqrt(DH_L))), 0.0)
    normalizer = jnp.sum(weights, axis=1, keepdims=True)
    normalizer = jnp.where(normalizer > 0, normalizer, 1.0)
    attended = jnp.dot(
        weights.astype(jnp.bfloat16), values, preferred_element_type=jnp.float32
    ) / normalizer
    lifted = jnp.dot(pooled, lift_ref[...], preferred_element_type=jnp.float32)
    patch_rows = (lifted + attended).astype(jnp.bfloat16)
    kept_ref[...] = patch_rows[:quota]
    leaving_ref[...] = patch_rows[quota:]


def project_kernel(
    own_ref, other_ref, gain_ref, w_ref, queries_ref, keep_ref, send_ref, scaled_ref
):
    core = lax.axis_index("core")
    zl = lax.axis_index("zl")
    rows = own_ref.shape[2]
    width = own_ref.shape[3]
    squares = jnp.zeros((rows, 128), jnp.float32)
    for block_ref, block_core in ((own_ref, core), (other_ref, 1 - core)):
        for x in range(X):
            for yh in range(Y_HI):
                block = block_ref[x, yh].astype(jnp.float32)
                first = pl.multiple_of((yh * X * CORE + x * CORE + block_core) * width, width)
                gain = gain_ref[:, pl.ds(first, width)]
                for lanes in range(0, width, 128):
                    piece = block[:, lanes : lanes + 128]
                    squares = squares + piece * piece
                scaled_ref[:, pl.ds(first, width)] = (block * gain).astype(jnp.bfloat16)
    total = jnp.dot(scaled_ref[...], w_ref[...], preferred_element_type=jnp.float32)
    row_scale = lax.rsqrt(jnp.sum(squares, axis=1, keepdims=True) / DG + 1e-05)
    total = (total * row_scale).astype(jnp.bfloat16)
    for head in range(2):
        queries = total[:, head * 3 * DH : head * 3 * DH + DH]
        for yy in range(Y_LO):
            queries_ref[2 * yy + head] = queries
        keys_vals = total[:, head * 3 * DH + DH : (head + 1) * 3 * DH]

        @pl.when(zl == head)
        def _():
            keep_ref[...] = keys_vals

        @pl.when(zl != head)
        def _():
            send_ref[...] = keys_vals


def attend_kernel(q_ref, kv_ref, out_ref, vt_ref, s_ref):
    y = lax.axis_index("yl")
    zh = lax.axis_index("zh")
    key_count = kv_ref.shape[0]
    rows = 2 * q_ref.shape[1]
    half = q_ref.shape[1]
    scale = 1.0 / math.sqrt(DH)
    vt_ref[...] = kv_ref[:, DH:].T
    chunk = 256

    def attend(yy, masked):
        queries = q_ref[pl.ds(2 * yy, 2)].reshape(rows, DH)
        peak = jnp.full((1, rows), neg_large, jnp.float32)
        for first in range(0, key_count, chunk):
            scores = lax.dot_general(
                kv_ref[first : first + chunk, :DH],
                queries,
                (((1,), (1,)), ((), ())),
                preferred_element_type=jnp.float32,
            )
            if masked:
                key_at = first + lax.broadcasted_iota(jnp.int32, scores.shape, 0)
                query_at = zh * rows + lax.broadcasted_iota(jnp.int32, scores.shape, 1)
                scores = jnp.where(key_at <= query_at, scores, neg_large)
            s_ref[first : first + chunk] = scores
            peak = jnp.maximum(peak, jnp.max(scores, axis=0, keepdims=True))
        normalizer = jnp.zeros((1, rows), jnp.float32)
        summed = jnp.zeros((DH, rows), jnp.float32)
        for first in range(0, key_count, chunk):
            weights = jnp.exp((s_ref[first : first + chunk] - peak) * scale)
            normalizer = normalizer + jnp.sum(weights, axis=0, keepdims=True)
            summed = summed + jnp.dot(
                vt_ref[:, first : first + chunk],
                weights.astype(jnp.bfloat16),
                preferred_element_type=jnp.float32,
            )
        summed = (summed / normalizer).astype(jnp.bfloat16)
        level = peak * scale + jnp.log(normalizer)
        high = level.astype(jnp.bfloat16)
        rest = level - high.astype(jnp.float32)
        mid = rest.astype(jnp.bfloat16)
        low = (rest - mid.astype(jnp.float32)).astype(jnp.bfloat16)
        stats = jnp.concatenate(
            [high, mid, low, jnp.zeros((13, rows), jnp.bfloat16)], axis=0
        )
        for part in range(2):
            lanes = slice(part * half, (part + 1) * half)
            out_ref[2 * yy + part, :DH, :] = summed[:, lanes]
            out_ref[2 * yy + part, DH:, :] = stats[:, lanes]

    for yy in range(Y_LO):

        @pl.when(yy < y)
        def _():
            row_at = lax.broadcasted_iota(jnp.int32, (16, half), 0)
            stats = jnp.where(row_at == 0, neg_large, 0.0).astype(jnp.bfloat16)
            for part in range(2):
                out_ref[2 * yy + part, :DH, :] = jnp.zeros((DH, half), jnp.bfloat16)
                out_ref[2 * yy + part, DH:, :] = stats

        @pl.when(yy == y)
        def _():
            attend(yy, True)

        @pl.when(yy > y)
        def _():
            attend(yy, False)


def merge_kernel(parts_ref, out_ref):
    for head in range(2):
        levels = []
        for yy in range(Y_LO):
            stats = parts_ref[2 * yy + head, DH:, :].astype(jnp.float32)
            levels.append(stats[0:1] + stats[1:2] + stats[2:3])
        peak = functools.reduce(jnp.maximum, levels)
        total = jnp.zeros((DH, out_ref.shape[0]), jnp.float32)
        normalizer = jnp.zeros((1, out_ref.shape[0]), jnp.float32)
        for yy in range(Y_LO):
            share = jnp.exp(levels[yy] - peak)
            normalizer = normalizer + share
            total = total + share * parts_ref[2 * yy + head, :DH, :].astype(jnp.float32)
        out_ref[:, head * DH : (head + 1) * DH] = (total / normalizer).T.astype(jnp.bfloat16)


VMEM = pl.BlockSpec(memory_space=pltpu.VMEM)


def all_to_all_of(block, axes):
    return lax.all_to_all(block, axes, 0, 0, tiled=True)


def local(enc_states, local_gain, w_local, w_cross, w_patch, byte_patch, global_gain, w_global):
    byte_count = enc_states.shape[0]
    quota = byte_count // PATCH_LEN
    half = byte_count // 2
    zl = lax.axis_index("zl")
    w_rows = jnp.transpose(w_local.reshape(w_local.shape[0], 3 * DH_L))
    model = enc_states.shape[1]
    HBM = pl.BlockSpec(memory_space=pltpu.HBM)
    held = [
        pltpu.VMEM((4, half // 4, model), jnp.bfloat16),
        pltpu.VMEM((half, model), jnp.bfloat16),
        pltpu.VMEM((1, model), jnp.float32),
        pltpu.VMEM((3 * DH_L, model), jnp.bfloat16),
    ]
    window_scratch = [
        pltpu.VMEM((byte_count, DH_L), jnp.bfloat16),
        pltpu.VMEM((DH_L, byte_count), jnp.bfloat16),
    ]
    gain_row = local_gain.reshape(1, -1)
    rim_shape = (2 * DH_L, half)
    late_queries, rim_sent = pl.pallas_call(
        second_half_kernel,
        out_shape=[
            jax.ShapeDtypeStruct((DH_L, half), jnp.bfloat16),
            jax.ShapeDtypeStruct(rim_shape, jnp.bfloat16),
        ],
        in_specs=[HBM] * 3,
        out_specs=[VMEM] * 2,
        scratch_shapes=held + [pltpu.SemaphoreType.DMA((6,))],
        compiler_params=pltpu.CompilerParams(vmem_limit_bytes=59 << 20),
        name="second_half",
    )(enc_states, gain_row, w_rows)
    rim = passed_along(rim_sent, CTX, 1)
    first_proj, late_out = pl.pallas_call(
        first_half_kernel,
        out_shape=[
            jax.ShapeDtypeStruct((3 * DH_L, half), jnp.bfloat16),
            jax.ShapeDtypeStruct((half, DH_L), jnp.bfloat16),
        ],
        in_specs=[HBM] * 5,
        out_specs=[VMEM] * 2,
        scratch_shapes=held
        + [pltpu.VMEM((DH_L, half), jnp.bfloat16), pltpu.VMEM(rim_shape, jnp.bfloat16)]
        + window_scratch
        + [pltpu.SemaphoreType.DMA((8,))],
        compiler_params=pltpu.CompilerParams(vmem_limit_bytes=59 << 20),
        cost_estimate=pl.CostEstimate(
            flops=2 * half * byte_count * 3 * DH_L + 4 * half * byte_count * DH_L,
            bytes_accessed=8 << 20,
            transcendentals=half * byte_count,
        ),
        name="first_half",
    )(enc_states, gain_row, w_rows, late_queries, rim_sent)
    kept_rows, leaving = pl.pallas_call(
        patch_kernel,
        out_shape=[jax.ShapeDtypeStruct((quota, w_patch.shape[2]), jnp.bfloat16)] * 2,
        in_specs=[HBM] * 6,
        out_specs=[VMEM, VMEM],
        scratch_shapes=[
            pltpu.VMEM(rim_shape, jnp.bfloat16),
            pltpu.VMEM((3 * DH_L, half), jnp.bfloat16),
            pltpu.VMEM((1, byte_count), jnp.int32),
            pltpu.VMEM(w_cross.shape[1:], jnp.bfloat16),
            pltpu.VMEM(w_patch.shape[1:], jnp.bfloat16),
        ]
        + window_scratch
        + [pltpu.VMEM((byte_count, DH_L), jnp.bfloat16), pltpu.SemaphoreType.DMA((6,))],
        compiler_params=pltpu.CompilerParams(vmem_limit_bytes=59 << 20),
        name="patches",
    )(rim, first_proj, late_out, byte_patch.reshape(1, -1), w_cross[0], w_patch[0])
    slab_rows = kept_rows + passed_along(leaving, CTX, 1)
    head_total = w_global.shape[1]
    flat_weight = w_global.reshape(DG, head_total * 3 * DH)
    slab_rows, flat_weight = lax.optimization_barrier((slab_rows, flat_weight))
    pair_rows = lax.all_gather(slab_rows, "yh", axis=0)
    own_rows = all_to_all_of(jnp.broadcast_to(pair_rows[None], (X,) + pair_rows.shape), "x")
    other_rows = lax.ppermute(own_rows, "core", [(0, 1), (1, 0)])
    queries, kept_kv, sent_kv = pl.pallas_call(
        project_kernel,
        out_shape=[
            jax.ShapeDtypeStruct((Y_LO * Z_PAIR, quota, DH), jnp.bfloat16),
            jax.ShapeDtypeStruct((quota, 2 * DH), jnp.bfloat16),
            jax.ShapeDtypeStruct((quota, 2 * DH), jnp.bfloat16),
        ],
        in_specs=[VMEM] * 4,
        out_specs=[VMEM, VMEM, VMEM],
        scratch_shapes=[pltpu.VMEM((quota, DG), jnp.bfloat16)],
        compiler_params=pltpu.CompilerParams(vmem_limit_bytes=32 << 20),
        cost_estimate=pl.CostEstimate(
            flops=2 * quota * DG * head_total * 3 * DH, bytes_accessed=8 << 20, transcendentals=0
        ),
        name="project",
    )(own_rows, other_rows, global_gain.reshape(1, DG), flat_weight)
    swapped = lax.ppermute(sent_kv, "zl", [(0, 1), (1, 0)])
    queries = all_to_all_of(queries, ("yl", "zl"))
    pair_kv = jnp.concatenate(
        [jnp.where(zl == 0, kept_kv, swapped), jnp.where(zl == 0, swapped, kept_kv)], axis=0
    )
    keys_vals = lax.all_gather(pair_kv, "zh", axis=0, tiled=True)
    key_count = keys_vals.shape[0]
    partial_out = pl.pallas_call(
        attend_kernel,
        out_shape=jax.ShapeDtypeStruct((Y_LO * Z_PAIR, DH + 16, quota), jnp.bfloat16),
        in_specs=[VMEM, VMEM],
        out_specs=VMEM,
        scratch_shapes=[
            pltpu.VMEM((DH, key_count), jnp.bfloat16),
            pltpu.VMEM((key_count, 2 * quota), jnp.float32),
        ],
        compiler_params=pltpu.CompilerParams(vmem_limit_bytes=32 << 20),
        name="attend",
    )(queries, keys_vals)
    parts = all_to_all_of(partial_out, ("yl", "zl"))
    return pl.pallas_call(
        merge_kernel,
        out_shape=jax.ShapeDtypeStruct((quota, head_total * DH), jnp.bfloat16),
        in_specs=[VMEM],
        out_specs=VMEM,
        compiler_params=pltpu.CompilerParams(vmem_limit_bytes=8 << 20),
        name="merge",
    )(parts)


def solution(mesh):
    split = Mesh(
        mesh.devices.reshape(Y_LO, Z_HALF, Z_PAIR, Y_HI, X, CORE), CTX + HEAD
    )
    in_specs = (
        P(CTX, None),
        P(),
        P(None, HEAD, None),
        P(HEAD, None, None),
        P(HEAD, None, None),
        P(CTX),
        P(),
        P(None, HEAD, None),
    )
    out_specs = P(CTX, HEAD)
    return jax.shard_map(local, mesh=split, in_specs=in_specs, out_specs=out_specs, check_vma=False)
```

```python
import functools
import math

import jax
import jax.numpy as jnp
from jax import lax
from jax.experimental import pallas as pl
from jax.experimental.pallas import tpu as pltpu
from jax.sharding import Mesh, PartitionSpec as P

CTX = ("yl", "zh", "zl")
HEAD = ("yh", "x", "core")
Y_LO, Z_HALF, Z_PAIR, Y_HI, X, CORE = 4, 6, 2, 2, 4, 2
N_CTX = Y_LO * Z_HALF * Z_PAIR

DH_L = 64
DH = 128
PATCH_LEN = 8
DG = 4096


neg_large = -1e30


def passed_along(block, axis, distance):
    devices = range(N_CTX)
    route = [(i - distance, i) for i in devices if i - distance in devices]
    return lax.ppermute(block, axis, route)


def rows_arriving(states_ref, held_ref, sems, first_row):
    step = held_ref.shape[1]
    copies = []
    for part in range(held_ref.shape[0]):
        rows = pl.ds(first_row + part * step, step)
        copy = pltpu.make_async_copy(states_ref.at[rows], held_ref.at[part], sems.at[part])
        copy.start()
        copies.append(copy)
    return copies


def norm_rows(states_ref, gain_ref, normed_ref):
    step = 32
    gain = gain_ref[...]
    for first in range(0, states_ref.shape[0], step):
        states = states_ref[first : first + step].astype(jnp.float32)
        scale = lax.rsqrt(jnp.mean(states * states, axis=1, keepdims=True) + 1e-05)
        normed_ref[first : first + step] = (states * scale * gain).astype(jnp.bfloat16)


def project_rows(weight_ref, normed_ref):
    return lax.dot_general(
        weight_ref[...], normed_ref[...], (((1,), (1,)), ((), ())), preferred_element_type=jnp.float32
    ).astype(jnp.bfloat16)


def second_half_kernel(
    states_ref, gain_hbm, w_hbm, query_ref, rim_ref, held_ref, normed_ref, gain_ref, w_ref, sems
):
    half = query_ref.shape[1]
    parts = held_ref.shape[0]
    gain_copy = pltpu.make_async_copy(gain_hbm, gain_ref, sems.at[parts])
    gain_copy.start()
    copies = rows_arriving(states_ref, held_ref, sems, half)
    w_copy = pltpu.make_async_copy(w_hbm, w_ref, sems.at[parts + 1])
    w_copy.start()
    gain_copy.wait()
    step = held_ref.shape[1]
    for part, copy in enumerate(copies):
        copy.wait()
        norm_rows(held_ref.at[part], gain_ref, normed_ref.at[pl.ds(part * step, step)])
    w_copy.wait()
    proj = project_rows(w_ref, normed_ref)
    query_ref[...] = proj[:DH_L]
    rim_ref[...] = proj[DH_L:]


def window_attend(queries_t, keys_ref, values_ref, early_bias, out_ref):
    scale = 1.0 / math.sqrt(DH_L)
    width = 128
    blocks = range(queries_t.shape[1] // width)
    row_at = lax.broadcasted_iota(jnp.int32, (width, width), 0)
    col_at = lax.broadcasted_iota(jnp.int32, (width, width), 1)
    scores = []
    for block in blocks:
        block_scores = []
        queries = queries_t[:, block * width : (block + 1) * width]
        for part in range(5):
            at = (block + part) * width
            part_scores = jnp.dot(
                keys_ref[at : at + width], queries, preferred_element_type=jnp.float32
            )
            if part == 0:
                part_scores = jnp.where(row_at > col_at, part_scores, neg_large)
            if part == 4:
                part_scores = jnp.where(row_at <= col_at, part_scores, neg_large)
            if early_bias is not None and at < keys_ref.shape[0] // 2:
                part_scores = part_scores + early_bias
            block_scores.append(part_scores)
        scores.append(block_scores)
    weights = []
    normalizers = []
    for block in blocks:
        peak = jnp.max(functools.reduce(jnp.maximum, scores[block]), axis=0, keepdims=True)
        block_weights = [jnp.exp((part_scores - peak) * scale) for part_scores in scores[block]]
        normalizers.append(
            jnp.sum(functools.reduce(jnp.add, block_weights), axis=0, keepdims=True)
        )
        weights.append(
            jnp.concatenate([part.astype(jnp.bfloat16) for part in block_weights], axis=0)
        )
    summed = [
        jnp.dot(
            values_ref[:, block * width : (block + 5) * width],
            weights[block],
            preferred_element_type=jnp.float32,
        )
        for block in blocks
    ]
    for block in blocks:
        out_ref[block * width : (block + 1) * width] = (
            summed[block] / normalizers[block]
        ).T.astype(jnp.bfloat16)


def started(pairs, sems, first):
    copies = [
        pltpu.make_async_copy(source, target, sems.at[first + at])
        for at, (source, target) in enumerate(pairs)
    ]
    for copy in copies:
        copy.start()
    return copies


def first_half_kernel(
    states_ref, gain_hbm, w_hbm, query_hbm, second_hbm, first_ref, out_ref,
    held_ref, normed_ref, gain_ref, w_ref, query_ref, second_ref, keys_ref, values_ref, sems,
):
    half = first_ref.shape[1]
    parts = held_ref.shape[0]
    step = held_ref.shape[1]
    (gain_copy,) = started(((gain_hbm, gain_ref),), sems, parts)
    copies = rows_arriving(states_ref, held_ref, sems, 0)
    others = started(
        ((second_hbm, second_ref), (w_hbm, w_ref), (query_hbm, query_ref)), sems, parts + 1
    )
    gain_copy.wait()
    for part, copy in enumerate(copies):
        copy.wait()
        norm_rows(held_ref.at[part], gain_ref, normed_ref.at[pl.ds(part * step, step)])
    for copy in others:
        copy.wait()
    keys_ref[half:] = second_ref[:DH_L].T
    values_ref[:, half:] = second_ref[DH_L:]
    proj = project_rows(w_ref, normed_ref)
    first_ref[...] = proj
    keys_ref[:half] = proj[DH_L : 2 * DH_L].T
    values_ref[:, :half] = proj[2 * DH_L :]
    window_attend(query_ref[...], keys_ref, values_ref, None, out_ref)


def patch_kernel(
    rim_hbm, first_hbm, late_hbm, patch_hbm, cross_hbm, lift_hbm, kept_ref, leaving_ref,
    rim_ref, first_ref, late_ref, patch_ref, cross_ref, lift_ref,
    keys_ref, values_ref, early_ref, local_ref, sems,
):
    ctx = lax.axis_index(CTX)
    half = first_ref.shape[1]
    copies = started(
        (
            (rim_hbm, rim_ref),
            (first_hbm, first_ref),
            (late_hbm, late_ref),
            (patch_hbm, patch_ref),
            (cross_hbm, cross_ref),
            (lift_hbm, lift_ref),
        ),
        sems,
        0,
    )
    local_ref[:, DH_L:] = jnp.ones((2 * half, DH_L), jnp.bfloat16)
    for copy in copies[:2]:
        copy.wait()
    rim_bias = jnp.where(ctx > 0, 0.0, neg_large).astype(jnp.float32)
    keys_ref[:half] = rim_ref[:DH_L].T
    keys_ref[half:] = first_ref[DH_L : 2 * DH_L].T
    values_ref[:, :half] = rim_ref[DH_L:]
    values_ref[:, half:] = first_ref[2 * DH_L :]
    window_attend(first_ref[:DH_L], keys_ref, values_ref, rim_bias, early_ref)
    for copy in copies[2:]:
        copy.wait()
    local_ref[:half, :DH_L] = early_ref[...]
    local_ref[half:, :DH_L] = late_ref[...]
    local_out = local_ref[:, :DH_L]
    quota = kept_ref.shape[0]
    slots = 2 * quota
    slot_of = patch_ref[...] - ctx * quota
    member = slot_of == lax.broadcasted_iota(jnp.int32, (slots, 2 * half), 0)
    member_f = jnp.where(member, 1.0, 0.0).astype(jnp.bfloat16)
    pooled = jnp.dot(member_f, local_ref[...], preferred_element_type=jnp.float32)
    counts = pooled[:, DH_L : DH_L + 1]
    pooled = (pooled[:, :DH_L] / jnp.maximum(counts, 1.0)).astype(jnp.bfloat16)
    keys = jnp.dot(
        local_out, cross_ref[:, :DH_L], preferred_element_type=jnp.float32
    ).astype(jnp.bfloat16)
    values = jnp.dot(
        local_out, cross_ref[:, DH_L:], preferred_element_type=jnp.float32
    ).astype(jnp.bfloat16)
    scores = lax.dot_general(
        pooled, keys, (((1,), (1,)), ((), ())), preferred_element_type=jnp.float32
    )
    scores = jnp.where(member, scores, neg_large)
    peak = jnp.maximum(jnp.max(scores, axis=1, keepdims=True), 0.1 * neg_large)
    weights = jnp.exp((scores - peak) * (1.0 / math.sqrt(DH_L)))
    normalizer = jnp.sum(weights, axis=1, keepdims=True)
    normalizer = jnp.where(normalizer > 0, normalizer, 1.0)
    attended = jnp.dot(
        weights.astype(jnp.bfloat16), values, preferred_element_type=jnp.float32
    ) / normalizer
    lifted = jnp.dot(pooled, lift_ref[...], preferred_element_type=jnp.float32)
    patch_rows = (lifted + attended).astype(jnp.bfloat16)
    kept_ref[...] = patch_rows[:quota]
    leaving_ref[...] = patch_rows[quota:]


def project_part(block_ref, block_core, gain_ref, w_ref, scaled_ref):
    rows = block_ref.shape[2]
    width = block_ref.shape[3]
    squares = jnp.zeros((rows, 128), jnp.float32)
    for yh in range(Y_HI):
        for x in range(X):
            block = block_ref[x, yh].astype(jnp.float32)
            place = yh * X + x
            first = pl.multiple_of((place * CORE + block_core) * width, width)
            for lanes in range(0, width, 128):
                piece = block[:, lanes : lanes + 128]
                squares = squares + piece * piece
            scaled_ref[:, place * width : (place + 1) * width] = (
                block * gain_ref[:, pl.ds(first, width)]
            ).astype(jnp.bfloat16)
    weight = w_ref[:, block_core].reshape(scaled_ref.shape[1], w_ref.shape[3])
    return jnp.dot(scaled_ref[...], weight, preferred_element_type=jnp.float32), squares


def project_own_kernel(own_ref, gain_ref, w_ref, total_ref, squares_ref, scaled_ref):
    core = lax.axis_index("core")
    total, squares = project_part(own_ref, core, gain_ref, w_ref, scaled_ref)
    total_ref[...] = total
    squares_ref[...] = squares


def project_other_kernel(
    own_total_ref, own_squares_ref, other_ref, gain_ref, w_ref,
    queries_ref, keep_ref, send_ref, scaled_ref,
):
    core = lax.axis_index("core")
    zl = lax.axis_index("zl")
    rows = send_ref.shape[0]
    total, squares = project_part(other_ref, 1 - core, gain_ref, w_ref, scaled_ref)
    total = total + own_total_ref[...]
    squares = squares + own_squares_ref[...]
    row_scale = lax.rsqrt(jnp.sum(squares, axis=1, keepdims=True) / DG + 1e-05)
    total = (total * row_scale).astype(jnp.bfloat16)
    for head in range(2):
        queries = total[:, head * 3 * DH : head * 3 * DH + DH]
        for yy in range(Y_LO):
            queries_ref[2 * yy + head] = queries
        keys_vals = total[:, head * 3 * DH + DH : (head + 1) * 3 * DH]

        @pl.when(zl == head)
        def _():
            keep_ref[head * rows : (head + 1) * rows] = keys_vals

        @pl.when(zl != head)
        def _():
            send_ref[...] = keys_vals


def attend_kernel(q_ref, kv_ref, out_ref, vt_ref, s_ref, p_ref):
    y = lax.axis_index("yl")
    zh = lax.axis_index("zh")
    key_count = kv_ref.shape[0]
    rows = 2 * q_ref.shape[1]
    half = q_ref.shape[1]
    scale = 1.0 / math.sqrt(DH)
    vt_ref[...] = kv_ref[:, DH:].T
    chunk = 256

    def attend(yy, last):
        reach = key_count if last is None else (last + 1) * chunk
        queries = q_ref[pl.ds(2 * yy, 2)].reshape(rows, DH)
        peak = jnp.full((8, rows), neg_large, jnp.float32)
        for first in range(0, reach, chunk):
            scores = lax.dot_general(
                kv_ref[first : first + chunk, :DH],
                queries,
                (((1,), (1,)), ((), ())),
                preferred_element_type=jnp.float32,
            )
            if last is not None and first == last * chunk:
                key_at = lax.broadcasted_iota(jnp.int32, scores.shape, 0)
                query_at = lax.broadcasted_iota(jnp.int32, scores.shape, 1)
                scores = jnp.where(key_at <= query_at, scores, neg_large)
            s_ref[first : first + chunk] = scores
            peak = jnp.maximum(peak, jnp.max(scores.reshape(chunk // 8, 8, rows), axis=0))
        peak = jnp.max(peak, axis=0, keepdims=True)
        normalizer = jnp.zeros((8, rows), jnp.float32)
        for first in range(0, reach, chunk):
            weights = jnp.exp((s_ref[first : first + chunk] - peak) * scale)
            normalizer = normalizer + jnp.sum(weights.reshape(chunk // 8, 8, rows), axis=0)
            p_ref[first : first + chunk] = weights.astype(jnp.bfloat16)
        normalizer = jnp.sum(normalizer, axis=0, keepdims=True)
        summed = jnp.dot(vt_ref[:, :reach], p_ref[:reach], preferred_element_type=jnp.float32)
        summed = (summed / normalizer).astype(jnp.bfloat16)
        level = peak * scale + jnp.log(normalizer)
        high = level.astype(jnp.bfloat16)
        rest = level - high.astype(jnp.float32)
        mid = rest.astype(jnp.bfloat16)
        low = (rest - mid.astype(jnp.float32)).astype(jnp.bfloat16)
        stats = jnp.concatenate(
            [high, mid, low, jnp.zeros((13, rows), jnp.bfloat16)], axis=0
        )
        for part in range(2):
            lanes = slice(part * half, (part + 1) * half)
            out_ref[2 * yy + part, :DH, :] = summed[:, lanes]
            out_ref[2 * yy + part, DH:, :] = stats[:, lanes]

    for yy in range(Y_LO):

        @pl.when(yy < y)
        def _():
            row_at = lax.broadcasted_iota(jnp.int32, (16, half), 0)
            stats = jnp.where(row_at == 0, neg_large, 0.0).astype(jnp.bfloat16)
            for part in range(2):
                out_ref[2 * yy + part, :DH, :] = jnp.zeros((DH, half), jnp.bfloat16)
                out_ref[2 * yy + part, DH:, :] = stats

        @pl.when(yy > y)
        def _():
            attend(yy, None)

    for last in range(Z_HALF):

        @pl.when(zh == last)
        def _():
            attend(y, last)


def merge_kernel(parts_ref, out_ref):
    for head in range(2):
        levels = []
        for yy in range(Y_LO):
            stats = parts_ref[2 * yy + head, DH:, :].astype(jnp.float32)
            levels.append(stats[0:1] + stats[1:2] + stats[2:3])
        peak = functools.reduce(jnp.maximum, levels)
        total = jnp.zeros((DH, out_ref.shape[0]), jnp.float32)
        normalizer = jnp.zeros((1, out_ref.shape[0]), jnp.float32)
        for yy in range(Y_LO):
            share = jnp.exp(levels[yy] - peak)
            normalizer = normalizer + share
            total = total + share * parts_ref[2 * yy + head, :DH, :].astype(jnp.float32)
        out_ref[:, head * DH : (head + 1) * DH] = (total / normalizer).T.astype(jnp.bfloat16)


VMEM = pl.BlockSpec(memory_space=pltpu.VMEM)


def all_to_all_of(block, axes):
    return lax.all_to_all(block, axes, 0, 0, tiled=True)


def local(enc_states, local_gain, w_local, w_cross, w_patch, byte_patch, global_gain, w_global):
    byte_count = enc_states.shape[0]
    quota = byte_count // PATCH_LEN
    half = byte_count // 2
    zl = lax.axis_index("zl")
    w_rows = jnp.transpose(w_local.reshape(w_local.shape[0], 3 * DH_L))
    model = enc_states.shape[1]
    HBM = pl.BlockSpec(memory_space=pltpu.HBM)
    held = [
        pltpu.VMEM((4, half // 4, model), jnp.bfloat16),
        pltpu.VMEM((half, model), jnp.bfloat16),
        pltpu.VMEM((1, model), jnp.float32),
        pltpu.VMEM((3 * DH_L, model), jnp.bfloat16),
    ]
    window_scratch = [
        pltpu.VMEM((byte_count, DH_L), jnp.bfloat16),
        pltpu.VMEM((DH_L, byte_count), jnp.bfloat16),
    ]
    gain_row = local_gain.reshape(1, -1)
    rim_shape = (2 * DH_L, half)
    late_queries, rim_sent = pl.pallas_call(
        second_half_kernel,
        out_shape=[
            jax.ShapeDtypeStruct((DH_L, half), jnp.bfloat16),
            jax.ShapeDtypeStruct(rim_shape, jnp.bfloat16),
        ],
        in_specs=[HBM] * 3,
        out_specs=[VMEM] * 2,
        scratch_shapes=held + [pltpu.SemaphoreType.DMA((6,))],
        compiler_params=pltpu.CompilerParams(vmem_limit_bytes=59 << 20),
        name="second_half",
    )(enc_states, gain_row, w_rows)
    rim = passed_along(rim_sent, CTX, 1)
    first_proj, late_out = pl.pallas_call(
        first_half_kernel,
        out_shape=[
            jax.ShapeDtypeStruct((3 * DH_L, half), jnp.bfloat16),
            jax.ShapeDtypeStruct((half, DH_L), jnp.bfloat16),
        ],
        in_specs=[HBM] * 5,
        out_specs=[VMEM] * 2,
        scratch_shapes=held
        + [pltpu.VMEM((DH_L, half), jnp.bfloat16), pltpu.VMEM(rim_shape, jnp.bfloat16)]
        + window_scratch
        + [pltpu.SemaphoreType.DMA((8,))],
        compiler_params=pltpu.CompilerParams(vmem_limit_bytes=59 << 20),
        cost_estimate=pl.CostEstimate(
            flops=2 * half * byte_count * 3 * DH_L + 4 * half * byte_count * DH_L,
            bytes_accessed=8 << 20,
            transcendentals=half * byte_count,
        ),
        name="first_half",
    )(enc_states, gain_row, w_rows, late_queries, rim_sent)
    kept_rows, leaving = pl.pallas_call(
        patch_kernel,
        out_shape=[jax.ShapeDtypeStruct((quota, w_patch.shape[2]), jnp.bfloat16)] * 2,
        in_specs=[HBM] * 6,
        out_specs=[VMEM, VMEM],
        scratch_shapes=[
            pltpu.VMEM(rim_shape, jnp.bfloat16),
            pltpu.VMEM((3 * DH_L, half), jnp.bfloat16),
            pltpu.VMEM((half, DH_L), jnp.bfloat16),
            pltpu.VMEM((1, byte_count), jnp.int32),
            pltpu.VMEM(w_cross.shape[1:], jnp.bfloat16),
            pltpu.VMEM(w_patch.shape[1:], jnp.bfloat16),
        ]
        + window_scratch
        + [
            pltpu.VMEM((half, DH_L), jnp.bfloat16),
            pltpu.VMEM((byte_count, 2 * DH_L), jnp.bfloat16),
            pltpu.SemaphoreType.DMA((6,)),
        ],
        compiler_params=pltpu.CompilerParams(vmem_limit_bytes=59 << 20),
        name="patches",
    )(rim, first_proj, late_out, byte_patch.reshape(1, -1), w_cross[0], w_patch[0])
    slab_rows = kept_rows + passed_along(leaving, CTX, 1)
    head_total = w_global.shape[1]
    flat_weight = w_global.reshape(DG, head_total * 3 * DH)
    slab_rows, flat_weight = lax.optimization_barrier((slab_rows, flat_weight))
    pair_rows = lax.all_gather(slab_rows, "yh", axis=0)
    own_rows = all_to_all_of(jnp.broadcast_to(pair_rows[None], (X,) + pair_rows.shape), "x")
    other_rows = lax.ppermute(own_rows, "core", [(0, 1), (1, 0)])
    out_width = head_total * 3 * DH
    split_weight = flat_weight.reshape(Y_HI * X, CORE, DG // (Y_HI * X * CORE), out_width)
    gain_all = global_gain.reshape(1, DG)
    cost = pl.CostEstimate(
        flops=quota * DG * out_width, bytes_accessed=4 << 20, transcendentals=0
    )
    scaled_scratch = [pltpu.VMEM((quota, DG // CORE), jnp.bfloat16)]
    own_total, own_squares = pl.pallas_call(
        project_own_kernel,
        out_shape=[
            jax.ShapeDtypeStruct((quota, out_width), jnp.float32),
            jax.ShapeDtypeStruct((quota, 128), jnp.float32),
        ],
        in_specs=[VMEM] * 3,
        out_specs=[VMEM] * 2,
        scratch_shapes=scaled_scratch,
        compiler_params=pltpu.CompilerParams(vmem_limit_bytes=32 << 20),
        cost_estimate=cost,
        name="project_own",
    )(own_rows, gain_all, split_weight)
    queries, kept_kv, sent_kv = pl.pallas_call(
        project_other_kernel,
        out_shape=[
            jax.ShapeDtypeStruct((Y_LO * Z_PAIR, quota, DH), jnp.bfloat16),
            jax.ShapeDtypeStruct((2 * quota, 2 * DH), jnp.bfloat16),
            jax.ShapeDtypeStruct((quota, 2 * DH), jnp.bfloat16),
        ],
        in_specs=[VMEM] * 5,
        out_specs=[VMEM] * 3,
        scratch_shapes=scaled_scratch,
        compiler_params=pltpu.CompilerParams(vmem_limit_bytes=32 << 20),
        cost_estimate=cost,
        name="project_other",
    )(own_total, own_squares, other_rows, gain_all, split_weight)
    swapped = lax.ppermute(sent_kv, "zl", [(0, 1), (1, 0)])
    queries = all_to_all_of(queries, ("yl", "zl"))
    pair_kv = lax.dynamic_update_slice_in_dim(kept_kv, swapped, (1 - zl) * quota, 0)
    keys_vals = lax.all_gather(pair_kv, "zh", axis=0, tiled=True)
    key_count = keys_vals.shape[0]
    partial_out = pl.pallas_call(
        attend_kernel,
        out_shape=jax.ShapeDtypeStruct((Y_LO * Z_PAIR, DH + 16, quota), jnp.bfloat16),
        in_specs=[VMEM, VMEM],
        out_specs=VMEM,
        scratch_shapes=[
            pltpu.VMEM((DH, key_count), jnp.bfloat16),
            pltpu.VMEM((key_count, 2 * quota), jnp.float32),
            pltpu.VMEM((key_count, 2 * quota), jnp.bfloat16),
        ],
        compiler_params=pltpu.CompilerParams(vmem_limit_bytes=32 << 20),
        name="attend",
    )(queries, keys_vals)
    parts = all_to_all_of(partial_out, ("yl", "zl"))
    return pl.pallas_call(
        merge_kernel,
        out_shape=jax.ShapeDtypeStruct((quota, head_total * DH), jnp.bfloat16),
        in_specs=[VMEM],
        out_specs=VMEM,
        compiler_params=pltpu.CompilerParams(vmem_limit_bytes=8 << 20),
        name="merge",
    )(parts)


def solution(mesh):
    split = Mesh(
        mesh.devices.reshape(Y_LO, Z_HALF, Z_PAIR, Y_HI, X, CORE), CTX + HEAD
    )
    in_specs = (
        P(CTX, None),
        P(),
        P(None, HEAD, None),
        P(HEAD, None, None),
        P(HEAD, None, None),
        P(CTX),
        P(),
        P(None, HEAD, None),
    )
    out_specs = P(CTX, HEAD)
    return jax.shard_map(local, mesh=split, in_specs=in_specs, out_specs=out_specs, check_vma=False)
```

```python
import functools
import math

import jax
import jax.numpy as jnp
from jax import lax
from jax.experimental import pallas as pl
from jax.experimental.pallas import tpu as pltpu
from jax.sharding import Mesh, PartitionSpec as P

CTX = ("yl", "zh", "zl")
HEAD = ("yh", "x", "core")
Y_LO, Z_HALF, Z_PAIR, Y_HI, X, CORE = 4, 6, 2, 2, 4, 2
N_CTX = Y_LO * Z_HALF * Z_PAIR

DH_L = 64
DH = 128
PATCH_LEN = 8
DG = 4096


neg_large = -1e30


def passed_along(block, axis, distance):
    devices = range(N_CTX)
    route = [(i - distance, i) for i in devices if i - distance in devices]
    return lax.ppermute(block, axis, route)


def rows_arriving(states_ref, held_ref, sems, first_row):
    step = held_ref.shape[1]
    copies = []
    for part in range(held_ref.shape[0]):
        rows = pl.ds(first_row + part * step, step)
        copy = pltpu.make_async_copy(states_ref.at[rows], held_ref.at[part], sems.at[part])
        copy.start()
        copies.append(copy)
    return copies


def norm_rows(states_ref, gain_ref, normed_ref):
    step = 32
    gain = gain_ref[...]
    for first in range(0, states_ref.shape[0], step):
        states = states_ref[first : first + step].astype(jnp.float32)
        scale = lax.rsqrt(jnp.mean(states * states, axis=1, keepdims=True) + 1e-05)
        normed_ref[first : first + step] = (states * scale * gain).astype(jnp.bfloat16)


def project_rows(weight_ref, normed_ref):
    return lax.dot_general(
        weight_ref[...], normed_ref[...], (((1,), (1,)), ((), ())), preferred_element_type=jnp.float32
    ).astype(jnp.bfloat16)


def second_half_kernel(
    states_ref, gain_hbm, w_hbm, query_ref, rim_ref, held_ref, normed_ref, gain_ref, w_ref, sems
):
    half = query_ref.shape[1]
    parts = held_ref.shape[0]
    gain_copy = pltpu.make_async_copy(gain_hbm, gain_ref, sems.at[parts])
    gain_copy.start()
    copies = rows_arriving(states_ref, held_ref, sems, half)
    w_copy = pltpu.make_async_copy(w_hbm, w_ref, sems.at[parts + 1])
    w_copy.start()
    gain_copy.wait()
    step = held_ref.shape[1]
    for part, copy in enumerate(copies):
        copy.wait()
        norm_rows(held_ref.at[part], gain_ref, normed_ref.at[pl.ds(part * step, step)])
    w_copy.wait()
    proj = project_rows(w_ref, normed_ref)
    query_ref[...] = proj[:DH_L]
    rim_ref[...] = proj[DH_L:]


def window_attend(queries_t, keys_ref, values_ref, early_bias, out_ref):
    scale = 1.0 / math.sqrt(DH_L)
    width = 128
    blocks = range(queries_t.shape[1] // width)
    row_at = lax.broadcasted_iota(jnp.int32, (width, width), 0)
    col_at = lax.broadcasted_iota(jnp.int32, (width, width), 1)
    scores = []
    for block in blocks:
        block_scores = []
        queries = queries_t[:, block * width : (block + 1) * width]
        for part in range(5):
            at = (block + part) * width
            part_scores = jnp.dot(
                keys_ref[at : at + width], queries, preferred_element_type=jnp.float32
            )
            if part == 0:
                part_scores = jnp.where(row_at > col_at, part_scores, neg_large)
            if part == 4:
                part_scores = jnp.where(row_at <= col_at, part_scores, neg_large)
            if early_bias is not None and at < keys_ref.shape[0] // 2:
                part_scores = part_scores + early_bias
            block_scores.append(part_scores)
        scores.append(block_scores)
    weights = []
    normalizers = []
    for block in blocks:
        peak = jnp.max(functools.reduce(jnp.maximum, scores[block]), axis=0, keepdims=True)
        block_weights = [jnp.exp((part_scores - peak) * scale) for part_scores in scores[block]]
        normalizers.append(
            jnp.sum(functools.reduce(jnp.add, block_weights), axis=0, keepdims=True)
        )
        weights.append(
            jnp.concatenate([part.astype(jnp.bfloat16) for part in block_weights], axis=0)
        )
    summed = [
        jnp.dot(
            values_ref[:, block * width : (block + 5) * width],
            weights[block],
            preferred_element_type=jnp.float32,
        )
        for block in blocks
    ]
    for block in blocks:
        out_ref[block * width : (block + 1) * width] = (
            summed[block] / normalizers[block]
        ).T.astype(jnp.bfloat16)


def started(pairs, sems, first):
    copies = [
        pltpu.make_async_copy(source, target, sems.at[first + at])
        for at, (source, target) in enumerate(pairs)
    ]
    for copy in copies:
        copy.start()
    return copies


def first_half_kernel(
    states_ref, gain_hbm, w_hbm, query_hbm, second_hbm, first_ref, out_ref,
    held_ref, normed_ref, gain_ref, w_ref, query_ref, second_ref, keys_ref, values_ref, sems,
):
    half = first_ref.shape[1]
    parts = held_ref.shape[0]
    step = held_ref.shape[1]
    (gain_copy,) = started(((gain_hbm, gain_ref),), sems, parts)
    copies = rows_arriving(states_ref, held_ref, sems, 0)
    others = started(
        ((second_hbm, second_ref), (w_hbm, w_ref), (query_hbm, query_ref)), sems, parts + 1
    )
    gain_copy.wait()
    for part, copy in enumerate(copies):
        copy.wait()
        norm_rows(held_ref.at[part], gain_ref, normed_ref.at[pl.ds(part * step, step)])
    for copy in others:
        copy.wait()
    keys_ref[half:] = second_ref[:DH_L].T
    values_ref[:, half:] = second_ref[DH_L:]
    proj = project_rows(w_ref, normed_ref)
    first_ref[...] = proj
    keys_ref[:half] = proj[DH_L : 2 * DH_L].T
    values_ref[:, :half] = proj[2 * DH_L :]
    window_attend(query_ref[...], keys_ref, values_ref, None, out_ref)


def patch_kernel(
    rim_hbm, first_hbm, late_hbm, patch_hbm, cross_hbm, lift_hbm, kept_ref, leaving_ref,
    rim_ref, first_ref, late_ref, patch_ref, cross_ref, lift_ref,
    keys_ref, values_ref, early_ref, local_ref, sems,
):
    ctx = lax.axis_index(CTX)
    half = first_ref.shape[1]
    copies = started(
        (
            (rim_hbm, rim_ref),
            (first_hbm, first_ref),
            (late_hbm, late_ref),
            (patch_hbm, patch_ref),
            (cross_hbm, cross_ref),
            (lift_hbm, lift_ref),
        ),
        sems,
        0,
    )
    local_ref[:, DH_L:] = jnp.ones((2 * half, DH_L), jnp.bfloat16)
    for copy in copies[:2]:
        copy.wait()
    rim_bias = jnp.where(ctx > 0, 0.0, neg_large).astype(jnp.float32)
    keys_ref[:half] = rim_ref[:DH_L].T
    keys_ref[half:] = first_ref[DH_L : 2 * DH_L].T
    values_ref[:, :half] = rim_ref[DH_L:]
    values_ref[:, half:] = first_ref[2 * DH_L :]
    window_attend(first_ref[:DH_L], keys_ref, values_ref, rim_bias, early_ref)
    for copy in copies[2:]:
        copy.wait()
    local_ref[:half, :DH_L] = early_ref[...]
    local_ref[half:, :DH_L] = late_ref[...]
    local_out = local_ref[:, :DH_L]
    quota = kept_ref.shape[0]
    slots = 2 * quota
    slot_of = patch_ref[...] - ctx * quota
    member = slot_of == lax.broadcasted_iota(jnp.int32, (slots, 2 * half), 0)
    member_f = jnp.where(member, 1.0, 0.0).astype(jnp.bfloat16)
    pooled = jnp.dot(member_f, local_ref[...], preferred_element_type=jnp.float32)
    counts = pooled[:, DH_L : DH_L + 1]
    pooled = (pooled[:, :DH_L] / jnp.maximum(counts, 1.0)).astype(jnp.bfloat16)
    keys = jnp.dot(
        local_out, cross_ref[:, :DH_L], preferred_element_type=jnp.float32
    ).astype(jnp.bfloat16)
    values = jnp.dot(
        local_out, cross_ref[:, DH_L:], preferred_element_type=jnp.float32
    ).astype(jnp.bfloat16)
    scores = lax.dot_general(
        pooled, keys, (((1,), (1,)), ((), ())), preferred_element_type=jnp.float32
    )
    scores = jnp.where(member, scores, neg_large)
    peak = jnp.maximum(jnp.max(scores, axis=1, keepdims=True), 0.1 * neg_large)
    weights = jnp.exp((scores - peak) * (1.0 / math.sqrt(DH_L)))
    normalizer = jnp.sum(weights, axis=1, keepdims=True)
    normalizer = jnp.where(normalizer > 0, normalizer, 1.0)
    attended = jnp.dot(
        weights.astype(jnp.bfloat16), values, preferred_element_type=jnp.float32
    ) / normalizer
    lifted = jnp.dot(pooled, lift_ref[...], preferred_element_type=jnp.float32)
    patch_rows = (lifted + attended).astype(jnp.bfloat16)
    kept_ref[...] = patch_rows[:quota]
    leaving_ref[...] = patch_rows[quota:]


def project_part(block_ref, block_core, gain_ref, w_ref, scaled_ref):
    rows = block_ref.shape[2]
    width = block_ref.shape[3]
    squares = jnp.zeros((rows, 128), jnp.float32)
    for yh in range(Y_HI):
        for x in range(X):
            block = block_ref[x, yh].astype(jnp.float32)
            place = yh * X + x
            first = pl.multiple_of((place * CORE + block_core) * width, width)
            for lanes in range(0, width, 128):
                piece = block[:, lanes : lanes + 128]
                squares = squares + piece * piece
            scaled_ref[:, place * width : (place + 1) * width] = (
                block * gain_ref[:, pl.ds(first, width)]
            ).astype(jnp.bfloat16)
    weight = w_ref[:, block_core].reshape(scaled_ref.shape[1], w_ref.shape[3])
    return jnp.dot(scaled_ref[...], weight, preferred_element_type=jnp.float32), squares


def project_own_kernel(own_ref, gain_ref, w_ref, total_ref, squares_ref, scaled_ref):
    core = lax.axis_index("core")
    total, squares = project_part(own_ref, core, gain_ref, w_ref, scaled_ref)
    total_ref[...] = total
    squares_ref[...] = squares


def project_other_kernel(
    own_total_ref, own_squares_ref, other_ref, gain_ref, w_ref,
    queries_ref, keep_ref, send_ref, scaled_ref,
):
    core = lax.axis_index("core")
    zl = lax.axis_index("zl")
    total, squares = project_part(other_ref, 1 - core, gain_ref, w_ref, scaled_ref)
    total = total + own_total_ref[...]
    squares = squares + own_squares_ref[...]
    row_scale = lax.rsqrt(jnp.sum(squares, axis=1, keepdims=True) / DG + 1e-05)
    total = (total * row_scale).astype(jnp.bfloat16)
    for head in range(2):
        queries = total[:, head * 3 * DH : head * 3 * DH + DH]
        for yy in range(Y_LO):
            queries_ref[2 * yy + head] = queries
        keys_vals = total[:, head * 3 * DH + DH : (head + 1) * 3 * DH]

        @pl.when(zl == head)
        def _():
            keep_ref[...] = keys_vals

        @pl.when(zl != head)
        def _():
            send_ref[...] = keys_vals


def attend_kernel(q_ref, kv_ref, out_ref, vt_ref, s_ref, p_ref):
    y = lax.axis_index("yl")
    zh = lax.axis_index("zh")
    key_count = kv_ref.shape[0]
    rows = 2 * q_ref.shape[1]
    half = q_ref.shape[1]
    scale = 1.0 / math.sqrt(DH)
    vt_ref[...] = kv_ref[:, DH:].T
    chunk = 256

    def attend(yy, last):
        reach = key_count if last is None else (last + 1) * chunk
        slot = 0 if last is not None else yy % 2
        queries = q_ref[pl.ds(2 * yy, 2)].reshape(rows, DH)
        peak = jnp.full((8, rows), neg_large, jnp.float32)
        for first in range(0, reach, chunk):
            scores = lax.dot_general(
                kv_ref[first : first + chunk, :DH],
                queries,
                (((1,), (1,)), ((), ())),
                preferred_element_type=jnp.float32,
            )
            if last is not None and first == last * chunk:
                key_at = lax.broadcasted_iota(jnp.int32, scores.shape, 0)
                query_at = lax.broadcasted_iota(jnp.int32, scores.shape, 1)
                scores = jnp.where(key_at <= query_at, scores, neg_large)
            s_ref[slot, first : first + chunk] = scores
            peak = jnp.maximum(peak, jnp.max(scores.reshape(chunk // 8, 8, rows), axis=0))
        peak = jnp.max(peak, axis=0, keepdims=True)
        normalizer = jnp.zeros((8, rows), jnp.float32)
        for first in range(0, reach, chunk):
            weights = jnp.exp((s_ref[slot, first : first + chunk] - peak) * scale)
            normalizer = normalizer + jnp.sum(weights.reshape(chunk // 8, 8, rows), axis=0)
            p_ref[slot, first : first + chunk] = weights.astype(jnp.bfloat16)
        normalizer = jnp.sum(normalizer, axis=0, keepdims=True)
        summed = jnp.dot(vt_ref[:, :reach], p_ref[slot, :reach], preferred_element_type=jnp.float32)
        summed = (summed / normalizer).astype(jnp.bfloat16)
        level = peak * scale + jnp.log(normalizer)
        high = level.astype(jnp.bfloat16)
        rest = level - high.astype(jnp.float32)
        mid = rest.astype(jnp.bfloat16)
        low = (rest - mid.astype(jnp.float32)).astype(jnp.bfloat16)
        stats = jnp.concatenate(
            [high, mid, low, jnp.zeros((13, rows), jnp.bfloat16)], axis=0
        )
        for part in range(2):
            lanes = slice(part * half, (part + 1) * half)
            out_ref[2 * yy + part, :DH, :] = summed[:, lanes]
            out_ref[2 * yy + part, DH:, :] = stats[:, lanes]

    for yy in range(Y_LO):

        @pl.when(yy < y)
        def _():
            row_at = lax.broadcasted_iota(jnp.int32, (16, half), 0)
            stats = jnp.where(row_at == 0, neg_large, 0.0).astype(jnp.bfloat16)
            for part in range(2):
                out_ref[2 * yy + part, :DH, :] = jnp.zeros((DH, half), jnp.bfloat16)
                out_ref[2 * yy + part, DH:, :] = stats

    for own in range(Y_LO - 1):

        @pl.when(y == own)
        def _():
            for yy in range(own + 1, Y_LO):
                attend(yy, None)

    for last in range(Z_HALF):

        @pl.when(zh == last)
        def _():
            attend(y, last)


def merge_kernel(parts_ref, out_ref):
    for head in range(2):
        levels = []
        for yy in range(Y_LO):
            stats = parts_ref[2 * yy + head, DH:, :].astype(jnp.float32)
            levels.append(stats[0:1] + stats[1:2] + stats[2:3])
        peak = functools.reduce(jnp.maximum, levels)
        total = jnp.zeros((DH, out_ref.shape[0]), jnp.float32)
        normalizer = jnp.zeros((1, out_ref.shape[0]), jnp.float32)
        for yy in range(Y_LO):
            share = jnp.exp(levels[yy] - peak)
            normalizer = normalizer + share
            total = total + share * parts_ref[2 * yy + head, :DH, :].astype(jnp.float32)
        out_ref[:, head * DH : (head + 1) * DH] = (total / normalizer).T.astype(jnp.bfloat16)


VMEM = pl.BlockSpec(memory_space=pltpu.VMEM)


def all_to_all_of(block, axes):
    return lax.all_to_all(block, axes, 0, 0, tiled=True)


def local(enc_states, local_gain, w_local, w_cross, w_patch, byte_patch, global_gain, w_global):
    byte_count = enc_states.shape[0]
    quota = byte_count // PATCH_LEN
    half = byte_count // 2
    zl = lax.axis_index("zl")
    w_rows = jnp.transpose(w_local.reshape(w_local.shape[0], 3 * DH_L))
    model = enc_states.shape[1]
    HBM = pl.BlockSpec(memory_space=pltpu.HBM)
    held = [
        pltpu.VMEM((4, half // 4, model), jnp.bfloat16),
        pltpu.VMEM((half, model), jnp.bfloat16),
        pltpu.VMEM((1, model), jnp.float32),
        pltpu.VMEM((3 * DH_L, model), jnp.bfloat16),
    ]
    window_scratch = [
        pltpu.VMEM((byte_count, DH_L), jnp.bfloat16),
        pltpu.VMEM((DH_L, byte_count), jnp.bfloat16),
    ]
    gain_row = local_gain.reshape(1, -1)
    rim_shape = (2 * DH_L, half)
    late_queries, rim_sent = pl.pallas_call(
        second_half_kernel,
        out_shape=[
            jax.ShapeDtypeStruct((DH_L, half), jnp.bfloat16),
            jax.ShapeDtypeStruct(rim_shape, jnp.bfloat16),
        ],
        in_specs=[HBM] * 3,
        out_specs=[VMEM] * 2,
        scratch_shapes=held + [pltpu.SemaphoreType.DMA((6,))],
        compiler_params=pltpu.CompilerParams(vmem_limit_bytes=59 << 20),
        name="second_half",
    )(enc_states, gain_row, w_rows)
    rim = passed_along(rim_sent, CTX, 1)
    first_proj, late_out = pl.pallas_call(
        first_half_kernel,
        out_shape=[
            jax.ShapeDtypeStruct((3 * DH_L, half), jnp.bfloat16),
            jax.ShapeDtypeStruct((half, DH_L), jnp.bfloat16),
        ],
        in_specs=[HBM] * 5,
        out_specs=[VMEM] * 2,
        scratch_shapes=held
        + [pltpu.VMEM((DH_L, half), jnp.bfloat16), pltpu.VMEM(rim_shape, jnp.bfloat16)]
        + window_scratch
        + [pltpu.SemaphoreType.DMA((8,))],
        compiler_params=pltpu.CompilerParams(vmem_limit_bytes=59 << 20),
        cost_estimate=pl.CostEstimate(
            flops=2 * half * byte_count * 3 * DH_L + 4 * half * byte_count * DH_L,
            bytes_accessed=8 << 20,
            transcendentals=half * byte_count,
        ),
        name="first_half",
    )(enc_states, gain_row, w_rows, late_queries, rim_sent)
    kept_rows, leaving = pl.pallas_call(
        patch_kernel,
        out_shape=[jax.ShapeDtypeStruct((quota, w_patch.shape[2]), jnp.bfloat16)] * 2,
        in_specs=[HBM] * 6,
        out_specs=[VMEM, VMEM],
        scratch_shapes=[
            pltpu.VMEM(rim_shape, jnp.bfloat16),
            pltpu.VMEM((3 * DH_L, half), jnp.bfloat16),
            pltpu.VMEM((half, DH_L), jnp.bfloat16),
            pltpu.VMEM((1, byte_count), jnp.int32),
            pltpu.VMEM(w_cross.shape[1:], jnp.bfloat16),
            pltpu.VMEM(w_patch.shape[1:], jnp.bfloat16),
        ]
        + window_scratch
        + [
            pltpu.VMEM((half, DH_L), jnp.bfloat16),
            pltpu.VMEM((byte_count, 2 * DH_L), jnp.bfloat16),
            pltpu.SemaphoreType.DMA((6,)),
        ],
        compiler_params=pltpu.CompilerParams(vmem_limit_bytes=59 << 20),
        name="patches",
    )(rim, first_proj, late_out, byte_patch.reshape(1, -1), w_cross[0], w_patch[0])
    slab_rows = kept_rows + passed_along(leaving, CTX, 1)
    head_total = w_global.shape[1]
    flat_weight = w_global.reshape(DG, head_total * 3 * DH)
    slab_rows, flat_weight = lax.optimization_barrier((slab_rows, flat_weight))
    pair_rows = lax.all_gather(slab_rows, "yh", axis=0)
    own_rows = all_to_all_of(jnp.broadcast_to(pair_rows[None], (X,) + pair_rows.shape), "x")
    other_rows = lax.ppermute(own_rows, "core", [(0, 1), (1, 0)])
    out_width = head_total * 3 * DH
    split_weight = flat_weight.reshape(Y_HI * X, CORE, DG // (Y_HI * X * CORE), out_width)
    gain_all = global_gain.reshape(1, DG)
    cost = pl.CostEstimate(
        flops=quota * DG * out_width, bytes_accessed=4 << 20, transcendentals=0
    )
    scaled_scratch = [pltpu.VMEM((quota, DG // CORE), jnp.bfloat16)]
    own_total, own_squares = pl.pallas_call(
        project_own_kernel,
        out_shape=[
            jax.ShapeDtypeStruct((quota, out_width), jnp.float32),
            jax.ShapeDtypeStruct((quota, 128), jnp.float32),
        ],
        in_specs=[VMEM] * 3,
        out_specs=[VMEM] * 2,
        scratch_shapes=scaled_scratch,
        compiler_params=pltpu.CompilerParams(vmem_limit_bytes=32 << 20),
        cost_estimate=cost,
        name="project_own",
    )(own_rows, gain_all, split_weight)
    queries, kept_kv, sent_kv = pl.pallas_call(
        project_other_kernel,
        out_shape=[
            jax.ShapeDtypeStruct((Y_LO * Z_PAIR, quota, DH), jnp.bfloat16),
            jax.ShapeDtypeStruct((quota, 2 * DH), jnp.bfloat16),
            jax.ShapeDtypeStruct((quota, 2 * DH), jnp.bfloat16),
        ],
        in_specs=[VMEM] * 5,
        out_specs=[VMEM] * 3,
        scratch_shapes=scaled_scratch,
        compiler_params=pltpu.CompilerParams(vmem_limit_bytes=32 << 20),
        cost_estimate=cost,
        name="project_other",
    )(own_total, own_squares, other_rows, gain_all, split_weight)
    swapped = lax.ppermute(sent_kv, "zl", [(0, 1), (1, 0)])
    queries = all_to_all_of(queries, ("yl", "zl"))
    pair_kv = jnp.concatenate(
        [jnp.where(zl == 0, kept_kv, swapped), jnp.where(zl == 0, swapped, kept_kv)], axis=0
    )
    keys_vals = lax.all_gather(pair_kv, "zh", axis=0, tiled=True)
    key_count = keys_vals.shape[0]
    partial_out = pl.pallas_call(
        attend_kernel,
        out_shape=jax.ShapeDtypeStruct((Y_LO * Z_PAIR, DH + 16, quota), jnp.bfloat16),
        in_specs=[VMEM, VMEM],
        out_specs=VMEM,
        scratch_shapes=[
            pltpu.VMEM((DH, key_count), jnp.bfloat16),
            pltpu.VMEM((2, key_count, 2 * quota), jnp.float32),
            pltpu.VMEM((2, key_count, 2 * quota), jnp.bfloat16),
        ],
        compiler_params=pltpu.CompilerParams(vmem_limit_bytes=32 << 20),
        name="attend",
    )(queries, keys_vals)
    parts = all_to_all_of(partial_out, ("yl", "zl"))
    return pl.pallas_call(
        merge_kernel,
        out_shape=jax.ShapeDtypeStruct((quota, head_total * DH), jnp.bfloat16),
        in_specs=[VMEM],
        out_specs=VMEM,
        compiler_params=pltpu.CompilerParams(vmem_limit_bytes=8 << 20),
        name="merge",
    )(parts)


def solution(mesh):
    split = Mesh(
        mesh.devices.reshape(Y_LO, Z_HALF, Z_PAIR, Y_HI, X, CORE), CTX + HEAD
    )
    in_specs = (
        P(CTX, None),
        P(),
        P(None, HEAD, None),
        P(HEAD, None, None),
        P(HEAD, None, None),
        P(CTX),
        P(),
        P(None, HEAD, None),
    )
    out_specs = P(CTX, HEAD)
    return jax.shard_map(local, mesh=split, in_specs=in_specs, out_specs=out_specs, check_vma=False)
```

```python
import functools
import math

import jax
import jax.numpy as jnp
from jax import lax
from jax.experimental import pallas as pl
from jax.experimental.pallas import tpu as pltpu
from jax.sharding import Mesh, PartitionSpec as P

CTX = ("yl", "zh", "zl")
HEAD = ("yh", "x", "core")
Y_LO, Z_HALF, Z_PAIR, Y_HI, X, CORE = 4, 6, 2, 2, 4, 2
N_CTX = Y_LO * Z_HALF * Z_PAIR

DH_L = 64
DH = 128
PATCH_LEN = 8
DG = 4096


neg_large = -1e30


def passed_along(block, axis, distance):
    devices = range(N_CTX)
    route = [(i - distance, i) for i in devices if i - distance in devices]
    return lax.ppermute(block, axis, route)


def rows_arriving(states_ref, held_ref, sems, first_row):
    step = held_ref.shape[1]
    copies = []
    for part in range(held_ref.shape[0]):
        rows = pl.ds(first_row + part * step, step)
        copy = pltpu.make_async_copy(states_ref.at[rows], held_ref.at[part], sems.at[part])
        copy.start()
        copies.append(copy)
    return copies


def norm_rows(states_ref, gain_ref, normed_ref):
    step = 32
    gain = gain_ref[...]
    for first in range(0, states_ref.shape[0], step):
        states = states_ref[first : first + step].astype(jnp.float32)
        scale = lax.rsqrt(jnp.mean(states * states, axis=1, keepdims=True) + 1e-05)
        normed_ref[first : first + step] = (states * scale * gain).astype(jnp.bfloat16)


def project_rows(weight_ref, normed_ref):
    return lax.dot_general(
        weight_ref[...], normed_ref[...], (((1,), (1,)), ((), ())), preferred_element_type=jnp.float32
    ).astype(jnp.bfloat16)


def second_half_kernel(
    states_ref, gain_hbm, w_hbm, query_ref, rim_ref, held_ref, normed_ref, gain_ref, w_ref, sems
):
    half = query_ref.shape[1]
    parts = held_ref.shape[0]
    gain_copy = pltpu.make_async_copy(gain_hbm, gain_ref, sems.at[parts])
    gain_copy.start()
    copies = rows_arriving(states_ref, held_ref, sems, half)
    w_copy = pltpu.make_async_copy(w_hbm, w_ref, sems.at[parts + 1])
    w_copy.start()
    gain_copy.wait()
    step = held_ref.shape[1]
    for part, copy in enumerate(copies):
        copy.wait()
        norm_rows(held_ref.at[part], gain_ref, normed_ref.at[pl.ds(part * step, step)])
    w_copy.wait()
    proj = project_rows(w_ref, normed_ref)
    query_ref[...] = proj[:DH_L]
    rim_ref[...] = proj[DH_L:]


def window_attend(queries_t, keys_ref, values_ref, early_bias, out_ref, features_first):
    scale = 1.0 / math.sqrt(DH_L)
    width = 128
    blocks = range(queries_t.shape[1] // width)
    row_at = lax.broadcasted_iota(jnp.int32, (width, width), 0)
    col_at = lax.broadcasted_iota(jnp.int32, (width, width), 1)
    scores = []
    for block in blocks:
        block_scores = []
        queries = queries_t[:, block * width : (block + 1) * width]
        for part in range(5):
            at = (block + part) * width
            part_scores = jnp.dot(
                keys_ref[at : at + width], queries, preferred_element_type=jnp.float32
            )
            if part == 0:
                part_scores = jnp.where(row_at > col_at, part_scores, neg_large)
            if part == 4:
                part_scores = jnp.where(row_at <= col_at, part_scores, neg_large)
            if early_bias is not None and at < keys_ref.shape[0] // 2:
                part_scores = part_scores + early_bias
            block_scores.append(part_scores)
        scores.append(block_scores)
    weights = []
    normalizers = []
    for block in blocks:
        peak = jnp.max(functools.reduce(jnp.maximum, scores[block]), axis=0, keepdims=True)
        block_weights = [jnp.exp((part_scores - peak) * scale) for part_scores in scores[block]]
        normalizers.append(
            jnp.sum(functools.reduce(jnp.add, block_weights), axis=0, keepdims=True)
        )
        weights.append(
            jnp.concatenate([part.astype(jnp.bfloat16) for part in block_weights], axis=0)
        )
    summed = [
        jnp.dot(
            values_ref[:, block * width : (block + 5) * width],
            weights[block],
            preferred_element_type=jnp.float32,
        )
        for block in blocks
    ]
    for block in blocks:
        attended = summed[block] / normalizers[block]
        lanes = slice(block * width, (block + 1) * width)
        if features_first:
            out_ref[:, lanes] = attended.astype(jnp.bfloat16)
        else:
            out_ref[lanes] = attended.T.astype(jnp.bfloat16)


def started(pairs, sems, first):
    copies = [
        pltpu.make_async_copy(source, target, sems.at[first + at])
        for at, (source, target) in enumerate(pairs)
    ]
    for copy in copies:
        copy.start()
    return copies


PACK_LATE = 3 * DH_L
PACK_SLOTS = PACK_LATE + DH_L
PACK_CROSS = PACK_SLOTS + 16
PACK_LIFT = PACK_CROSS + DH_L
PACK_END = PACK_LIFT + DH_L


def first_half_kernel(
    states_ref, gain_hbm, w_hbm, query_hbm, second_hbm, patch_hbm, cross_hbm, lift_hbm, packed_ref,
    held_ref, normed_ref, gain_ref, w_ref, query_ref, second_ref, patch_ref, cross_ref, lift_ref,
    keys_ref, values_ref, sems,
):
    half = packed_ref.shape[1]
    parts = held_ref.shape[0]
    step = held_ref.shape[1]
    (gain_copy,) = started(((gain_hbm, gain_ref),), sems, parts)
    copies = rows_arriving(states_ref, held_ref, sems, 0)
    others = started(
        (
            (second_hbm, second_ref),
            (w_hbm, w_ref),
            (query_hbm, query_ref),
            (patch_hbm, patch_ref),
            (cross_hbm, cross_ref),
            (lift_hbm, lift_ref),
        ),
        sems,
        parts + 1,
    )
    gain_copy.wait()
    for part, copy in enumerate(copies):
        copy.wait()
        norm_rows(held_ref.at[part], gain_ref, normed_ref.at[pl.ds(part * step, step)])
    for copy in others:
        copy.wait()
    keys_ref[half:] = second_ref[:DH_L].T
    values_ref[:, half:] = second_ref[DH_L:]
    proj = project_rows(w_ref, normed_ref)
    packed_ref[:PACK_LATE] = proj
    keys_ref[:half] = proj[DH_L : 2 * DH_L].T
    values_ref[:, :half] = proj[2 * DH_L :]
    slots = (patch_ref[...] - lax.axis_index(CTX) * (half // 4)).astype(jnp.float32)
    row_at = lax.broadcasted_iota(jnp.int32, (16, half), 0)
    packed_ref[PACK_SLOTS:PACK_CROSS] = jnp.where(
        row_at == 0, slots[:, :half], jnp.where(row_at == 1, slots[:, half:], 0.0)
    ).astype(jnp.bfloat16)
    packed_ref[PACK_CROSS:PACK_LIFT, : cross_ref.shape[1]] = cross_ref[...]
    packed_ref[PACK_LIFT:, : lift_ref.shape[1]] = lift_ref[...]
    window_attend(
        query_ref[...], keys_ref, values_ref, None, packed_ref.at[pl.ds(PACK_LATE, DH_L)], True
    )


def patch_kernel(
    rim_ref, packed_ref, kept_ref, leaving_ref, keys_ref, values_ref, early_ref, local_ref
):
    ctx = lax.axis_index(CTX)
    half = packed_ref.shape[1]
    local_ref[:, DH_L:] = jnp.ones((2 * half, DH_L), jnp.bfloat16)
    rim_bias = jnp.where(ctx > 0, 0.0, neg_large).astype(jnp.float32)
    keys_ref[:half] = rim_ref[:DH_L].T
    keys_ref[half:] = packed_ref[DH_L : 2 * DH_L].T
    values_ref[:, :half] = rim_ref[DH_L:]
    values_ref[:, half:] = packed_ref[2 * DH_L : PACK_LATE]
    window_attend(packed_ref[:DH_L], keys_ref, values_ref, rim_bias, early_ref, False)
    local_ref[:half, :DH_L] = early_ref[...]
    local_ref[half:, :DH_L] = packed_ref[PACK_LATE:PACK_SLOTS].T
    local_out = local_ref[:, :DH_L]
    quota = kept_ref.shape[0]
    slots = 2 * quota
    slot_rows = packed_ref[PACK_SLOTS:PACK_CROSS].astype(jnp.float32)
    slot_of = jnp.concatenate([slot_rows[0:1], slot_rows[1:2]], axis=1)
    member = slot_of == lax.broadcasted_iota(jnp.int32, (slots, 2 * half), 0).astype(jnp.float32)
    lift_width = kept_ref.shape[1]
    member_f = jnp.where(member, 1.0, 0.0).astype(jnp.bfloat16)
    pooled = jnp.dot(member_f, local_ref[...], preferred_element_type=jnp.float32)
    counts = pooled[:, DH_L : DH_L + 1]
    pooled = (pooled[:, :DH_L] / jnp.maximum(counts, 1.0)).astype(jnp.bfloat16)
    keys = jnp.dot(
        local_out, packed_ref[PACK_CROSS:PACK_LIFT, :DH_L], preferred_element_type=jnp.float32
    ).astype(jnp.bfloat16)
    values = jnp.dot(
        local_out,
        packed_ref[PACK_CROSS:PACK_LIFT, DH_L : DH_L + lift_width],
        preferred_element_type=jnp.float32,
    ).astype(jnp.bfloat16)
    scores = lax.dot_general(
        pooled, keys, (((1,), (1,)), ((), ())), preferred_element_type=jnp.float32
    )
    scores = jnp.where(member, scores, neg_large)
    peak = jnp.maximum(jnp.max(scores, axis=1, keepdims=True), 0.1 * neg_large)
    weights = jnp.exp((scores - peak) * (1.0 / math.sqrt(DH_L)))
    normalizer = jnp.sum(weights, axis=1, keepdims=True)
    normalizer = jnp.where(normalizer > 0, normalizer, 1.0)
    attended = jnp.dot(
        weights.astype(jnp.bfloat16), values, preferred_element_type=jnp.float32
    ) / normalizer
    lifted = jnp.dot(
        pooled, packed_ref[PACK_LIFT:PACK_END, :lift_width], preferred_element_type=jnp.float32
    )
    patch_rows = (lifted + attended).astype(jnp.bfloat16)
    kept_ref[...] = patch_rows[:quota]
    leaving_ref[...] = patch_rows[quota:]


def project_part(block_ref, block_core, gain_ref, w_ref, scaled_ref):
    rows = block_ref.shape[2]
    width = block_ref.shape[3]
    squares = jnp.zeros((rows, 128), jnp.float32)
    for yh in range(Y_HI):
        for x in range(X):
            block = block_ref[x, yh].astype(jnp.float32)
            place = yh * X + x
            first = pl.multiple_of((place * CORE + block_core) * width, width)
            for lanes in range(0, width, 128):
                piece = block[:, lanes : lanes + 128]
                squares = squares + piece * piece
            scaled_ref[:, place * width : (place + 1) * width] = (
                block * gain_ref[:, pl.ds(first, width)]
            ).astype(jnp.bfloat16)
    weight = w_ref[:, block_core].reshape(scaled_ref.shape[1], w_ref.shape[3])
    return jnp.dot(scaled_ref[...], weight, preferred_element_type=jnp.float32), squares


def project_own_kernel(own_ref, gain_ref, w_ref, total_ref, squares_ref, scaled_ref):
    core = lax.axis_index("core")
    total, squares = project_part(own_ref, core, gain_ref, w_ref, scaled_ref)
    total_ref[...] = total
    squares_ref[...] = squares


def project_other_kernel(
    own_total_ref, own_squares_ref, other_ref, gain_ref, w_ref,
    queries_ref, keep_ref, send_ref, scaled_ref,
):
    core = lax.axis_index("core")
    zl = lax.axis_index("zl")
    total, squares = project_part(other_ref, 1 - core, gain_ref, w_ref, scaled_ref)
    total = total + own_total_ref[...]
    squares = squares + own_squares_ref[...]
    row_scale = lax.rsqrt(jnp.sum(squares, axis=1, keepdims=True) / DG + 1e-05)
    total = (total * row_scale).astype(jnp.bfloat16)
    for head in range(2):
        queries = total[:, head * 3 * DH : head * 3 * DH + DH]
        for yy in range(Y_LO):
            queries_ref[2 * yy + head] = queries
        keys_vals = total[:, head * 3 * DH + DH : (head + 1) * 3 * DH]

        @pl.when(zl == head)
        def _():
            keep_ref[...] = keys_vals

        @pl.when(zl != head)
        def _():
            send_ref[...] = keys_vals


def attend_kernel(q_ref, kv_ref, out_ref, vt_ref, s_ref, p_ref):
    y = lax.axis_index("yl")
    zh = lax.axis_index("zh")
    key_count = kv_ref.shape[0]
    rows = 2 * q_ref.shape[1]
    half = q_ref.shape[1]
    scale = 1.0 / math.sqrt(DH)
    vt_ref[...] = kv_ref[:, DH:].T
    chunk = 256

    def attend(yy, last):
        reach = key_count if last is None else (last + 1) * chunk
        slot = 0 if last is not None else yy % 2
        queries = q_ref[pl.ds(2 * yy, 2)].reshape(rows, DH)
        peak = jnp.full((8, rows), neg_large, jnp.float32)
        for first in range(0, reach, chunk):
            scores = lax.dot_general(
                kv_ref[first : first + chunk, :DH],
                queries,
                (((1,), (1,)), ((), ())),
                preferred_element_type=jnp.float32,
            )
            if last is not None and first == last * chunk:
                key_at = lax.broadcasted_iota(jnp.int32, scores.shape, 0)
                query_at = lax.broadcasted_iota(jnp.int32, scores.shape, 1)
                scores = jnp.where(key_at <= query_at, scores, neg_large)
            s_ref[slot, first : first + chunk] = scores
            peak = jnp.maximum(peak, jnp.max(scores.reshape(chunk // 8, 8, rows), axis=0))
        peak = jnp.max(peak, axis=0, keepdims=True)
        normalizer = jnp.zeros((8, rows), jnp.float32)
        for first in range(0, reach, chunk):
            weights = jnp.exp((s_ref[slot, first : first + chunk] - peak) * scale)
            normalizer = normalizer + jnp.sum(weights.reshape(chunk // 8, 8, rows), axis=0)
            p_ref[slot, first : first + chunk] = weights.astype(jnp.bfloat16)
        normalizer = jnp.sum(normalizer, axis=0, keepdims=True)
        summed = jnp.dot(vt_ref[:, :reach], p_ref[slot, :reach], preferred_element_type=jnp.float32)
        summed = (summed / normalizer).astype(jnp.bfloat16)
        level = peak * scale + jnp.log(normalizer)
        high = level.astype(jnp.bfloat16)
        rest = level - high.astype(jnp.float32)
        mid = rest.astype(jnp.bfloat16)
        low = (rest - mid.astype(jnp.float32)).astype(jnp.bfloat16)
        stats = jnp.concatenate(
            [high, mid, low, jnp.zeros((13, rows), jnp.bfloat16)], axis=0
        )
        for part in range(2):
            lanes = slice(part * half, (part + 1) * half)
            out_ref[2 * yy + part, :DH, :] = summed[:, lanes]
            out_ref[2 * yy + part, DH:, :] = stats[:, lanes]

    for yy in range(Y_LO):

        @pl.when(yy < y)
        def _():
            row_at = lax.broadcasted_iota(jnp.int32, (16, half), 0)
            stats = jnp.where(row_at == 0, neg_large, 0.0).astype(jnp.bfloat16)
            for part in range(2):
                out_ref[2 * yy + part, :DH, :] = jnp.zeros((DH, half), jnp.bfloat16)
                out_ref[2 * yy + part, DH:, :] = stats

    for own in range(Y_LO - 1):

        @pl.when(y == own)
        def _():
            for yy in range(own + 1, Y_LO):
                attend(yy, None)

    for last in range(Z_HALF):

        @pl.when(zh == last)
        def _():
            attend(y, last)


def merge_kernel(parts_ref, out_ref):
    for head in range(2):
        levels = []
        for yy in range(Y_LO):
            stats = parts_ref[2 * yy + head, DH:, :].astype(jnp.float32)
            levels.append(stats[0:1] + stats[1:2] + stats[2:3])
        peak = functools.reduce(jnp.maximum, levels)
        total = jnp.zeros((DH, out_ref.shape[0]), jnp.float32)
        normalizer = jnp.zeros((1, out_ref.shape[0]), jnp.float32)
        for yy in range(Y_LO):
            share = jnp.exp(levels[yy] - peak)
            normalizer = normalizer + share
            total = total + share * parts_ref[2 * yy + head, :DH, :].astype(jnp.float32)
        out_ref[:, head * DH : (head + 1) * DH] = (total / normalizer).T.astype(jnp.bfloat16)


VMEM = pl.BlockSpec(memory_space=pltpu.VMEM)


def all_to_all_of(block, axes):
    return lax.all_to_all(block, axes, 0, 0, tiled=True)


def local(enc_states, local_gain, w_local, w_cross, w_patch, byte_patch, global_gain, w_global):
    byte_count = enc_states.shape[0]
    quota = byte_count // PATCH_LEN
    half = byte_count // 2
    zl = lax.axis_index("zl")
    w_rows = jnp.transpose(w_local.reshape(w_local.shape[0], 3 * DH_L))
    model = enc_states.shape[1]
    HBM = pl.BlockSpec(memory_space=pltpu.HBM)
    held = [
        pltpu.VMEM((4, half // 4, model), jnp.bfloat16),
        pltpu.VMEM((half, model), jnp.bfloat16),
        pltpu.VMEM((1, model), jnp.float32),
        pltpu.VMEM((3 * DH_L, model), jnp.bfloat16),
    ]
    window_scratch = [
        pltpu.VMEM((byte_count, DH_L), jnp.bfloat16),
        pltpu.VMEM((DH_L, byte_count), jnp.bfloat16),
    ]
    gain_row = local_gain.reshape(1, -1)
    rim_shape = (2 * DH_L, half)
    late_queries, rim_sent = pl.pallas_call(
        second_half_kernel,
        out_shape=[
            jax.ShapeDtypeStruct((DH_L, half), jnp.bfloat16),
            jax.ShapeDtypeStruct(rim_shape, jnp.bfloat16),
        ],
        in_specs=[HBM] * 3,
        out_specs=[VMEM] * 2,
        scratch_shapes=held + [pltpu.SemaphoreType.DMA((6,))],
        compiler_params=pltpu.CompilerParams(vmem_limit_bytes=59 << 20),
        name="second_half",
    )(enc_states, gain_row, w_rows)
    rim = passed_along(rim_sent, CTX, 1)
    packed = pl.pallas_call(
        first_half_kernel,
        out_shape=jax.ShapeDtypeStruct((PACK_END, half), jnp.bfloat16),
        in_specs=[HBM] * 8,
        out_specs=VMEM,
        scratch_shapes=held
        + [
            pltpu.VMEM((DH_L, half), jnp.bfloat16),
            pltpu.VMEM(rim_shape, jnp.bfloat16),
            pltpu.VMEM((1, byte_count), jnp.int32),
            pltpu.VMEM(w_cross.shape[1:], jnp.bfloat16),
            pltpu.VMEM(w_patch.shape[1:], jnp.bfloat16),
        ]
        + window_scratch
        + [pltpu.SemaphoreType.DMA((11,))],
        compiler_params=pltpu.CompilerParams(vmem_limit_bytes=59 << 20),
        cost_estimate=pl.CostEstimate(
            flops=2 * half * byte_count * 3 * DH_L + 4 * half * byte_count * DH_L,
            bytes_accessed=8 << 20,
            transcendentals=half * byte_count,
        ),
        name="first_half",
    )(
        enc_states, gain_row, w_rows, late_queries, rim_sent,
        byte_patch.reshape(1, -1), w_cross[0], w_patch[0],
    )
    kept_rows, leaving = pl.pallas_call(
        patch_kernel,
        out_shape=[jax.ShapeDtypeStruct((quota, w_patch.shape[2]), jnp.bfloat16)] * 2,
        in_specs=[VMEM] * 2,
        out_specs=[VMEM, VMEM],
        scratch_shapes=window_scratch
        + [
            pltpu.VMEM((half, DH_L), jnp.bfloat16),
            pltpu.VMEM((byte_count, 2 * DH_L), jnp.bfloat16),
        ],
        compiler_params=pltpu.CompilerParams(vmem_limit_bytes=24 << 20),
        name="patches",
    )(rim, packed)
    slab_rows = kept_rows + passed_along(leaving, CTX, 1)
    head_total = w_global.shape[1]
    flat_weight = w_global.reshape(DG, head_total * 3 * DH)
    slab_rows, flat_weight = lax.optimization_barrier((slab_rows, flat_weight))
    pair_rows = lax.all_gather(slab_rows, "yh", axis=0)
    own_rows = all_to_all_of(jnp.broadcast_to(pair_rows[None], (X,) + pair_rows.shape), "x")
    other_rows = lax.ppermute(own_rows, "core", [(0, 1), (1, 0)])
    out_width = head_total * 3 * DH
    split_weight = flat_weight.reshape(Y_HI * X, CORE, DG // (Y_HI * X * CORE), out_width)
    gain_all = global_gain.reshape(1, DG)
    cost = pl.CostEstimate(
        flops=quota * DG * out_width, bytes_accessed=4 << 20, transcendentals=0
    )
    scaled_scratch = [pltpu.VMEM((quota, DG // CORE), jnp.bfloat16)]
    own_total, own_squares = pl.pallas_call(
        project_own_kernel,
        out_shape=[
            jax.ShapeDtypeStruct((quota, out_width), jnp.float32),
            jax.ShapeDtypeStruct((quota, 128), jnp.float32),
        ],
        in_specs=[VMEM] * 3,
        out_specs=[VMEM] * 2,
        scratch_shapes=scaled_scratch,
        compiler_params=pltpu.CompilerParams(vmem_limit_bytes=32 << 20),
        cost_estimate=cost,
        name="project_own",
    )(own_rows, gain_all, split_weight)
    queries, kept_kv, sent_kv = pl.pallas_call(
        project_other_kernel,
        out_shape=[
            jax.ShapeDtypeStruct((Y_LO * Z_PAIR, quota, DH), jnp.bfloat16),
            jax.ShapeDtypeStruct((quota, 2 * DH), jnp.bfloat16),
            jax.ShapeDtypeStruct((quota, 2 * DH), jnp.bfloat16),
        ],
        in_specs=[VMEM] * 5,
        out_specs=[VMEM] * 3,
        scratch_shapes=scaled_scratch,
        compiler_params=pltpu.CompilerParams(vmem_limit_bytes=32 << 20),
        cost_estimate=cost,
        name="project_other",
    )(own_total, own_squares, other_rows, gain_all, split_weight)
    swapped = lax.ppermute(sent_kv, "zl", [(0, 1), (1, 0)])
    queries = all_to_all_of(queries, ("yl", "zl"))
    pair_kv = jnp.concatenate(
        [jnp.where(zl == 0, kept_kv, swapped), jnp.where(zl == 0, swapped, kept_kv)], axis=0
    )
    keys_vals = lax.all_gather(pair_kv, "zh", axis=0, tiled=True)
    key_count = keys_vals.shape[0]
    partial_out = pl.pallas_call(
        attend_kernel,
        out_shape=jax.ShapeDtypeStruct((Y_LO * Z_PAIR, DH + 16, quota), jnp.bfloat16),
        in_specs=[VMEM, VMEM],
        out_specs=VMEM,
        scratch_shapes=[
            pltpu.VMEM((DH, key_count), jnp.bfloat16),
            pltpu.VMEM((2, key_count, 2 * quota), jnp.float32),
            pltpu.VMEM((2, key_count, 2 * quota), jnp.bfloat16),
        ],
        compiler_params=pltpu.CompilerParams(vmem_limit_bytes=32 << 20),
        name="attend",
    )(queries, keys_vals)
    parts = all_to_all_of(partial_out, ("yl", "zl"))
    return pl.pallas_call(
        merge_kernel,
        out_shape=jax.ShapeDtypeStruct((quota, head_total * DH), jnp.bfloat16),
        in_specs=[VMEM],
        out_specs=VMEM,
        compiler_params=pltpu.CompilerParams(vmem_limit_bytes=8 << 20),
        name="merge",
    )(parts)


def solution(mesh):
    split = Mesh(
        mesh.devices.reshape(Y_LO, Z_HALF, Z_PAIR, Y_HI, X, CORE), CTX + HEAD
    )
    in_specs = (
        P(CTX, None),
        P(),
        P(None, HEAD, None),
        P(HEAD, None, None),
        P(HEAD, None, None),
        P(CTX),
        P(),
        P(None, HEAD, None),
    )
    out_specs = P(CTX, HEAD)
    return jax.shard_map(local, mesh=split, in_specs=in_specs, out_specs=out_specs, check_vma=False)
```

```python
import functools
import math

import jax
import jax.numpy as jnp
from jax import lax
from jax.experimental import pallas as pl
from jax.experimental.pallas import tpu as pltpu
from jax.sharding import Mesh, PartitionSpec as P

CTX = ("yl", "zh", "zl")
HEAD = ("yh", "x", "core")
Y_LO, Z_HALF, Z_PAIR, Y_HI, X, CORE = 4, 6, 2, 2, 4, 2
N_CTX = Y_LO * Z_HALF * Z_PAIR

DH_L = 64
DH = 128
PATCH_LEN = 8
DG = 4096


neg_large = -1e30


def passed_along(block, axis, distance):
    devices = range(N_CTX)
    route = [(i - distance, i) for i in devices if i - distance in devices]
    return lax.ppermute(block, axis, route)


def rows_arriving(states_ref, held_ref, sems, first_row):
    step = held_ref.shape[1]
    copies = []
    for part in range(held_ref.shape[0]):
        rows = pl.ds(first_row + part * step, step)
        copy = pltpu.make_async_copy(states_ref.at[rows], held_ref.at[part], sems.at[part])
        copy.start()
        copies.append(copy)
    return copies


def norm_rows(states_ref, gain_ref, normed_ref):
    step = 16
    gain = gain_ref[...]
    for first in range(0, states_ref.shape[0], step):
        states = states_ref[first : first + step].astype(jnp.float32)
        scale = lax.rsqrt(jnp.mean(states * states, axis=1, keepdims=True) + 1e-05)
        normed_ref[first : first + step] = (states * scale * gain).astype(jnp.bfloat16)


def project_rows(weight_ref, normed_ref):
    return lax.dot_general(
        weight_ref[...], normed_ref[...], (((1,), (1,)), ((), ())), preferred_element_type=jnp.float32
    ).astype(jnp.bfloat16)


def second_half_kernel(
    states_ref, gain_hbm, w_hbm, query_ref, rim_ref, held_ref, normed_ref, gain_ref, w_ref, sems
):
    half = query_ref.shape[1]
    parts = held_ref.shape[0]
    gain_copy = pltpu.make_async_copy(gain_hbm, gain_ref, sems.at[parts])
    gain_copy.start()
    copies = rows_arriving(states_ref, held_ref, sems, half)
    w_copy = pltpu.make_async_copy(w_hbm, w_ref, sems.at[parts + 1])
    w_copy.start()
    gain_copy.wait()
    step = held_ref.shape[1]
    for part, copy in enumerate(copies):
        copy.wait()
        norm_rows(held_ref.at[part], gain_ref, normed_ref.at[pl.ds(part * step, step)])
    w_copy.wait()
    proj = project_rows(w_ref, normed_ref)
    query_ref[...] = proj[:DH_L]
    rim_ref[...] = proj[DH_L:]


def window_attend(queries_t, keys_ref, values_ref, early_bias, out_ref, features_first):
    scale = 1.0 / math.sqrt(DH_L)
    width = 128
    blocks = range(queries_t.shape[1] // width)
    row_at = lax.broadcasted_iota(jnp.int32, (width, width), 0)
    col_at = lax.broadcasted_iota(jnp.int32, (width, width), 1)
    scores = []
    for block in blocks:
        block_scores = []
        queries = queries_t[:, block * width : (block + 1) * width]
        for part in range(5):
            at = (block + part) * width
            part_scores = jnp.dot(
                keys_ref[at : at + width], queries, preferred_element_type=jnp.float32
            )
            if part == 0:
                part_scores = jnp.where(row_at > col_at, part_scores, neg_large)
            if part == 4:
                part_scores = jnp.where(row_at <= col_at, part_scores, neg_large)
            if early_bias is not None and at < keys_ref.shape[0] // 2:
                part_scores = part_scores + early_bias
            block_scores.append(part_scores)
        scores.append(block_scores)
    weights = []
    normalizers = []
    for block in blocks:
        peak = jnp.max(functools.reduce(jnp.maximum, scores[block]), axis=0, keepdims=True)
        block_weights = [jnp.exp((part_scores - peak) * scale) for part_scores in scores[block]]
        normalizers.append(
            jnp.sum(functools.reduce(jnp.add, block_weights), axis=0, keepdims=True)
        )
        weights.append(
            jnp.concatenate([part.astype(jnp.bfloat16) for part in block_weights], axis=0)
        )
    summed = [
        jnp.dot(
            values_ref[:, block * width : (block + 5) * width],
            weights[block],
            preferred_element_type=jnp.float32,
        )
        for block in blocks
    ]
    for block in blocks:
        attended = summed[block] / normalizers[block]
        lanes = slice(block * width, (block + 1) * width)
        if features_first:
            out_ref[:, lanes] = attended.astype(jnp.bfloat16)
        else:
            out_ref[lanes] = attended.T.astype(jnp.bfloat16)


def started(pairs, sems, first):
    copies = [
        pltpu.make_async_copy(source, target, sems.at[first + at])
        for at, (source, target) in enumerate(pairs)
    ]
    for copy in copies:
        copy.start()
    return copies


PACK_LATE = 3 * DH_L
PACK_SLOTS = PACK_LATE + DH_L
PACK_CROSS = PACK_SLOTS + 16
PACK_LIFT = PACK_CROSS + DH_L
PACK_END = PACK_LIFT + DH_L


def first_half_kernel(
    states_ref, gain_hbm, w_hbm, query_hbm, second_hbm, patch_hbm, cross_hbm, lift_hbm, packed_ref,
    held_ref, normed_ref, gain_ref, w_ref, query_ref, second_ref, patch_ref, cross_ref, lift_ref,
    keys_ref, values_ref, sems,
):
    half = packed_ref.shape[1]
    parts = held_ref.shape[0]
    step = held_ref.shape[1]
    (gain_copy,) = started(((gain_hbm, gain_ref),), sems, parts)
    copies = rows_arriving(states_ref, held_ref, sems, 0)
    others = started(
        (
            (second_hbm, second_ref),
            (w_hbm, w_ref),
            (query_hbm, query_ref),
            (patch_hbm, patch_ref),
            (cross_hbm, cross_ref),
            (lift_hbm, lift_ref),
        ),
        sems,
        parts + 1,
    )
    gain_copy.wait()
    for part, copy in enumerate(copies):
        copy.wait()
        norm_rows(held_ref.at[part], gain_ref, normed_ref.at[pl.ds(part * step, step)])
    for copy in others:
        copy.wait()
    keys_ref[half:] = second_ref[:DH_L].T
    values_ref[:, half:] = second_ref[DH_L:]
    proj = project_rows(w_ref, normed_ref)
    packed_ref[:PACK_LATE] = proj
    keys_ref[:half] = proj[DH_L : 2 * DH_L].T
    values_ref[:, :half] = proj[2 * DH_L :]
    slots = (patch_ref[...] - lax.axis_index(CTX) * (half // 4)).astype(jnp.float32)
    row_at = lax.broadcasted_iota(jnp.int32, (16, half), 0)
    packed_ref[PACK_SLOTS:PACK_CROSS] = jnp.where(
        row_at == 0, slots[:, :half], jnp.where(row_at == 1, slots[:, half:], 0.0)
    ).astype(jnp.bfloat16)
    packed_ref[PACK_CROSS:PACK_LIFT, : cross_ref.shape[1]] = cross_ref[...]
    packed_ref[PACK_LIFT:, : lift_ref.shape[1]] = lift_ref[...]
    window_attend(
        query_ref[...], keys_ref, values_ref, None, packed_ref.at[pl.ds(PACK_LATE, DH_L)], True
    )


def patch_kernel(
    rim_ref, packed_ref, kept_ref, leaving_ref, keys_ref, values_ref, early_ref, local_ref
):
    ctx = lax.axis_index(CTX)
    half = packed_ref.shape[1]
    local_ref[:, DH_L:] = jnp.ones((2 * half, DH_L), jnp.bfloat16)
    rim_bias = jnp.where(ctx > 0, 0.0, neg_large).astype(jnp.float32)
    keys_ref[:half] = rim_ref[:DH_L].T
    keys_ref[half:] = packed_ref[DH_L : 2 * DH_L].T
    values_ref[:, :half] = rim_ref[DH_L:]
    values_ref[:, half:] = packed_ref[2 * DH_L : PACK_LATE]
    window_attend(packed_ref[:DH_L], keys_ref, values_ref, rim_bias, early_ref, False)
    local_ref[:half, :DH_L] = early_ref[...]
    local_ref[half:, :DH_L] = packed_ref[PACK_LATE:PACK_SLOTS].T
    local_out = local_ref[:, :DH_L]
    quota = kept_ref.shape[0]
    slots = 2 * quota
    slot_rows = packed_ref[PACK_SLOTS:PACK_CROSS].astype(jnp.float32)
    slot_of = jnp.concatenate([slot_rows[0:1], slot_rows[1:2]], axis=1)
    member = slot_of == lax.broadcasted_iota(jnp.int32, (slots, 2 * half), 0).astype(jnp.float32)
    lift_width = kept_ref.shape[1]
    member_f = jnp.where(member, 1.0, 0.0).astype(jnp.bfloat16)
    pooled = jnp.dot(member_f, local_ref[...], preferred_element_type=jnp.float32)
    counts = pooled[:, DH_L : DH_L + 1]
    pooled = (pooled[:, :DH_L] / jnp.maximum(counts, 1.0)).astype(jnp.bfloat16)
    keys = jnp.dot(
        local_out, packed_ref[PACK_CROSS:PACK_LIFT, :DH_L], preferred_element_type=jnp.float32
    ).astype(jnp.bfloat16)
    values = jnp.dot(
        local_out,
        packed_ref[PACK_CROSS:PACK_LIFT, DH_L : DH_L + lift_width],
        preferred_element_type=jnp.float32,
    ).astype(jnp.bfloat16)
    scores = lax.dot_general(
        pooled, keys, (((1,), (1,)), ((), ())), preferred_element_type=jnp.float32
    )
    scores = jnp.where(member, scores, neg_large)
    peak = jnp.maximum(jnp.max(scores, axis=1, keepdims=True), 0.1 * neg_large)
    weights = jnp.exp((scores - peak) * (1.0 / math.sqrt(DH_L)))
    normalizer = jnp.sum(weights, axis=1, keepdims=True)
    normalizer = jnp.where(normalizer > 0, normalizer, 1.0)
    attended = jnp.dot(
        weights.astype(jnp.bfloat16), values, preferred_element_type=jnp.float32
    ) / normalizer
    lifted = jnp.dot(
        pooled, packed_ref[PACK_LIFT:PACK_END, :lift_width], preferred_element_type=jnp.float32
    )
    patch_rows = (lifted + attended).astype(jnp.bfloat16)
    kept_ref[...] = patch_rows[:quota]
    leaving_ref[...] = patch_rows[quota:]


def project_part(block_ref, block_core, gain_ref, w_ref, scaled_ref):
    rows = block_ref.shape[2]
    width = block_ref.shape[3]
    squares = jnp.zeros((rows, 128), jnp.float32)
    for yh in range(Y_HI):
        for x in range(X):
            block = block_ref[x, yh].astype(jnp.float32)
            place = yh * X + x
            first = pl.multiple_of((place * CORE + block_core) * width, width)
            for lanes in range(0, width, 128):
                piece = block[:, lanes : lanes + 128]
                squares = squares + piece * piece
            scaled_ref[:, place * width : (place + 1) * width] = (
                block * gain_ref[:, pl.ds(first, width)]
            ).astype(jnp.bfloat16)
    weight = w_ref[:, block_core].reshape(scaled_ref.shape[1], w_ref.shape[3])
    return jnp.dot(scaled_ref[...], weight, preferred_element_type=jnp.float32), squares


def project_own_kernel(own_ref, gain_ref, w_ref, total_ref, squares_ref, scaled_ref):
    core = lax.axis_index("core")
    total, squares = project_part(own_ref, core, gain_ref, w_ref, scaled_ref)
    total_ref[...] = total
    squares_ref[...] = squares


def project_other_kernel(
    own_total_ref, own_squares_ref, other_ref, gain_ref, w_ref,
    queries_ref, keep_ref, send_ref, scaled_ref,
):
    core = lax.axis_index("core")
    zl = lax.axis_index("zl")
    total, squares = project_part(other_ref, 1 - core, gain_ref, w_ref, scaled_ref)
    total = total + own_total_ref[...]
    squares = squares + own_squares_ref[...]
    row_scale = lax.rsqrt(jnp.sum(squares, axis=1, keepdims=True) / DG + 1e-05)
    total = (total * row_scale).astype(jnp.bfloat16)
    for head in range(2):
        queries = total[:, head * 3 * DH : head * 3 * DH + DH]
        for yy in range(Y_LO):
            queries_ref[2 * yy + head] = queries
        keys_vals = total[:, head * 3 * DH + DH : (head + 1) * 3 * DH]

        @pl.when(zl == head)
        def _():
            keep_ref[...] = keys_vals

        @pl.when(zl != head)
        def _():
            send_ref[...] = keys_vals


def attend_kernel(q_ref, kv_ref, out_ref, vt_ref, s_ref, p_ref):
    y = lax.axis_index("yl")
    zh = lax.axis_index("zh")
    key_count = kv_ref.shape[0]
    rows = 2 * q_ref.shape[1]
    half = q_ref.shape[1]
    scale = 1.0 / math.sqrt(DH)
    vt_ref[...] = kv_ref[:, DH:].T
    chunk = 256

    def attend(yy, last):
        reach = key_count if last is None else (last + 1) * chunk
        slot = 0 if last is not None else yy % 2
        queries = q_ref[pl.ds(2 * yy, 2)].reshape(rows, DH)
        peak = jnp.full((8, rows), neg_large, jnp.float32)
        for first in range(0, reach, chunk):
            scores = lax.dot_general(
                kv_ref[first : first + chunk, :DH],
                queries,
                (((1,), (1,)), ((), ())),
                preferred_element_type=jnp.float32,
            )
            if last is not None and first == last * chunk:
                key_at = lax.broadcasted_iota(jnp.int32, scores.shape, 0)
                query_at = lax.broadcasted_iota(jnp.int32, scores.shape, 1)
                scores = jnp.where(key_at <= query_at, scores, neg_large)
            s_ref[slot, first : first + chunk] = scores
            peak = jnp.maximum(peak, jnp.max(scores.reshape(chunk // 8, 8, rows), axis=0))
        peak = jnp.max(peak, axis=0, keepdims=True)
        normalizer = jnp.zeros((8, rows), jnp.float32)
        for first in range(0, reach, chunk):
            weights = jnp.exp((s_ref[slot, first : first + chunk] - peak) * scale)
            normalizer = normalizer + jnp.sum(weights.reshape(chunk // 8, 8, rows), axis=0)
            p_ref[slot, first : first + chunk] = weights.astype(jnp.bfloat16)
        normalizer = jnp.sum(normalizer, axis=0, keepdims=True)
        summed = jnp.dot(vt_ref[:, :reach], p_ref[slot, :reach], preferred_element_type=jnp.float32)
        summed = (summed / normalizer).astype(jnp.bfloat16)
        level = peak * scale + jnp.log(normalizer)
        high = level.astype(jnp.bfloat16)
        rest = level - high.astype(jnp.float32)
        mid = rest.astype(jnp.bfloat16)
        low = (rest - mid.astype(jnp.float32)).astype(jnp.bfloat16)
        stats = jnp.concatenate(
            [high, mid, low, jnp.zeros((13, rows), jnp.bfloat16)], axis=0
        )
        for part in range(2):
            lanes = slice(part * half, (part + 1) * half)
            out_ref[2 * yy + part, :DH, :] = summed[:, lanes]
            out_ref[2 * yy + part, DH:, :] = stats[:, lanes]

    for yy in range(Y_LO):

        @pl.when(yy < y)
        def _():
            row_at = lax.broadcasted_iota(jnp.int32, (16, half), 0)
            stats = jnp.where(row_at == 0, neg_large, 0.0).astype(jnp.bfloat16)
            for part in range(2):
                out_ref[2 * yy + part, :DH, :] = jnp.zeros((DH, half), jnp.bfloat16)
                out_ref[2 * yy + part, DH:, :] = stats

    for own in range(Y_LO - 1):

        @pl.when(y == own)
        def _():
            for yy in range(own + 1, Y_LO):
                attend(yy, None)

    for last in range(Z_HALF):

        @pl.when(zh == last)
        def _():
            attend(y, last)


def merge_kernel(parts_ref, out_ref):
    for head in range(2):
        levels = []
        for yy in range(Y_LO):
            stats = parts_ref[2 * yy + head, DH:, :].astype(jnp.float32)
            levels.append(stats[0:1] + stats[1:2] + stats[2:3])
        peak = functools.reduce(jnp.maximum, levels)
        total = jnp.zeros((DH, out_ref.shape[0]), jnp.float32)
        normalizer = jnp.zeros((1, out_ref.shape[0]), jnp.float32)
        for yy in range(Y_LO):
            share = jnp.exp(levels[yy] - peak)
            normalizer = normalizer + share
            total = total + share * parts_ref[2 * yy + head, :DH, :].astype(jnp.float32)
        out_ref[:, head * DH : (head + 1) * DH] = (total / normalizer).T.astype(jnp.bfloat16)


VMEM = pl.BlockSpec(memory_space=pltpu.VMEM)


def all_to_all_of(block, axes):
    return lax.all_to_all(block, axes, 0, 0, tiled=True)


def local(enc_states, local_gain, w_local, w_cross, w_patch, byte_patch, global_gain, w_global):
    byte_count = enc_states.shape[0]
    quota = byte_count // PATCH_LEN
    half = byte_count // 2
    zl = lax.axis_index("zl")
    w_rows = jnp.transpose(w_local.reshape(w_local.shape[0], 3 * DH_L))
    model = enc_states.shape[1]
    HBM = pl.BlockSpec(memory_space=pltpu.HBM)
    held = [
        pltpu.VMEM((2, half // 2, model), jnp.bfloat16),
        pltpu.VMEM((half, model), jnp.bfloat16),
        pltpu.VMEM((1, model), jnp.float32),
        pltpu.VMEM((3 * DH_L, model), jnp.bfloat16),
    ]
    window_scratch = [
        pltpu.VMEM((byte_count, DH_L), jnp.bfloat16),
        pltpu.VMEM((DH_L, byte_count), jnp.bfloat16),
    ]
    gain_row = local_gain.reshape(1, -1)
    rim_shape = (2 * DH_L, half)
    late_queries, rim_sent = pl.pallas_call(
        second_half_kernel,
        out_shape=[
            jax.ShapeDtypeStruct((DH_L, half), jnp.bfloat16),
            jax.ShapeDtypeStruct(rim_shape, jnp.bfloat16),
        ],
        in_specs=[HBM] * 3,
        out_specs=[VMEM] * 2,
        scratch_shapes=held + [pltpu.SemaphoreType.DMA((4,))],
        compiler_params=pltpu.CompilerParams(vmem_limit_bytes=59 << 20),
        name="second_half",
    )(enc_states, gain_row, w_rows)
    rim = passed_along(rim_sent, CTX, 1)
    packed = pl.pallas_call(
        first_half_kernel,
        out_shape=jax.ShapeDtypeStruct((PACK_END, half), jnp.bfloat16),
        in_specs=[HBM] * 8,
        out_specs=VMEM,
        scratch_shapes=held
        + [
            pltpu.VMEM((DH_L, half), jnp.bfloat16),
            pltpu.VMEM(rim_shape, jnp.bfloat16),
            pltpu.VMEM((1, byte_count), jnp.int32),
            pltpu.VMEM(w_cross.shape[1:], jnp.bfloat16),
            pltpu.VMEM(w_patch.shape[1:], jnp.bfloat16),
        ]
        + window_scratch
        + [pltpu.SemaphoreType.DMA((9,))],
        compiler_params=pltpu.CompilerParams(vmem_limit_bytes=59 << 20),
        cost_estimate=pl.CostEstimate(
            flops=2 * half * byte_count * 3 * DH_L + 4 * half * byte_count * DH_L,
            bytes_accessed=8 << 20,
            transcendentals=half * byte_count,
        ),
        name="first_half",
    )(
        enc_states, gain_row, w_rows, late_queries, rim_sent,
        byte_patch.reshape(1, -1), w_cross[0], w_patch[0],
    )
    kept_rows, leaving = pl.pallas_call(
        patch_kernel,
        out_shape=[jax.ShapeDtypeStruct((quota, w_patch.shape[2]), jnp.bfloat16)] * 2,
        in_specs=[VMEM] * 2,
        out_specs=[VMEM, VMEM],
        scratch_shapes=window_scratch
        + [
            pltpu.VMEM((half, DH_L), jnp.bfloat16),
            pltpu.VMEM((byte_count, 2 * DH_L), jnp.bfloat16),
        ],
        compiler_params=pltpu.CompilerParams(vmem_limit_bytes=24 << 20),
        name="patches",
    )(rim, packed)
    slab_rows = kept_rows + passed_along(leaving, CTX, 1)
    head_total = w_global.shape[1]
    flat_weight = w_global.reshape(DG, head_total * 3 * DH)
    slab_rows, flat_weight = lax.optimization_barrier((slab_rows, flat_weight))
    pair_rows = lax.all_gather(slab_rows, "yh", axis=0)
    own_rows = all_to_all_of(jnp.broadcast_to(pair_rows[None], (X,) + pair_rows.shape), "x")
    other_rows = lax.ppermute(own_rows, "core", [(0, 1), (1, 0)])
    out_width = head_total * 3 * DH
    split_weight = flat_weight.reshape(Y_HI * X, CORE, DG // (Y_HI * X * CORE), out_width)
    gain_all = global_gain.reshape(1, DG)
    cost = pl.CostEstimate(
        flops=quota * DG * out_width, bytes_accessed=4 << 20, transcendentals=0
    )
    scaled_scratch = [pltpu.VMEM((quota, DG // CORE), jnp.bfloat16)]
    own_total, own_squares = pl.pallas_call(
        project_own_kernel,
        out_shape=[
            jax.ShapeDtypeStruct((quota, out_width), jnp.float32),
            jax.ShapeDtypeStruct((quota, 128), jnp.float32),
        ],
        in_specs=[VMEM] * 3,
        out_specs=[VMEM] * 2,
        scratch_shapes=scaled_scratch,
        compiler_params=pltpu.CompilerParams(vmem_limit_bytes=32 << 20),
        cost_estimate=cost,
        name="project_own",
    )(own_rows, gain_all, split_weight)
    queries, kept_kv, sent_kv = pl.pallas_call(
        project_other_kernel,
        out_shape=[
            jax.ShapeDtypeStruct((Y_LO * Z_PAIR, quota, DH), jnp.bfloat16),
            jax.ShapeDtypeStruct((quota, 2 * DH), jnp.bfloat16),
            jax.ShapeDtypeStruct((quota, 2 * DH), jnp.bfloat16),
        ],
        in_specs=[VMEM] * 5,
        out_specs=[VMEM] * 3,
        scratch_shapes=scaled_scratch,
        compiler_params=pltpu.CompilerParams(vmem_limit_bytes=32 << 20),
        cost_estimate=cost,
        name="project_other",
    )(own_total, own_squares, other_rows, gain_all, split_weight)
    swapped = lax.ppermute(sent_kv, "zl", [(0, 1), (1, 0)])
    queries = all_to_all_of(queries, ("yl", "zl"))
    pair_kv = jnp.concatenate(
        [jnp.where(zl == 0, kept_kv, swapped), jnp.where(zl == 0, swapped, kept_kv)], axis=0
    )
    keys_vals = lax.all_gather(pair_kv, "zh", axis=0, tiled=True)
    key_count = keys_vals.shape[0]
    partial_out = pl.pallas_call(
        attend_kernel,
        out_shape=jax.ShapeDtypeStruct((Y_LO * Z_PAIR, DH + 16, quota), jnp.bfloat16),
        in_specs=[VMEM, VMEM],
        out_specs=VMEM,
        scratch_shapes=[
            pltpu.VMEM((DH, key_count), jnp.bfloat16),
            pltpu.VMEM((2, key_count, 2 * quota), jnp.float32),
            pltpu.VMEM((2, key_count, 2 * quota), jnp.bfloat16),
        ],
        compiler_params=pltpu.CompilerParams(vmem_limit_bytes=32 << 20),
        name="attend",
    )(queries, keys_vals)
    parts = all_to_all_of(partial_out, ("yl", "zl"))
    return pl.pallas_call(
        merge_kernel,
        out_shape=jax.ShapeDtypeStruct((quota, head_total * DH), jnp.bfloat16),
        in_specs=[VMEM],
        out_specs=VMEM,
        compiler_params=pltpu.CompilerParams(vmem_limit_bytes=8 << 20),
        name="merge",
    )(parts)


def solution(mesh):
    split = Mesh(
        mesh.devices.reshape(Y_LO, Z_HALF, Z_PAIR, Y_HI, X, CORE), CTX + HEAD
    )
    in_specs = (
        P(CTX, None),
        P(),
        P(None, HEAD, None),
        P(HEAD, None, None),
        P(HEAD, None, None),
        P(CTX),
        P(),
        P(None, HEAD, None),
    )
    out_specs = P(CTX, HEAD)
    return jax.shard_map(local, mesh=split, in_specs=in_specs, out_specs=out_specs, check_vma=False)
```
